32 devices in a mesh: gx: 4 (over z), gy: 8 (over y, x, core).
Axes of the slice: x: 2, y: 2, z: 4, core: 2. Of those that a mesh axis runs over, the one named last changes fastest.
Arguments:
- depth: float32 [1024, 128, 128], P(('gx', 'gy')), may hold values from 0.1 to 2
- discharge: float32 [1024, 2, 128, 128], P(('gx', 'gy')), may hold values from -3 to 3
- bed: float32 [1024, 128, 128], P(('gx', 'gy')), may hold values from -1.5 to 2.5
- friction: float32 [1024, 128, 128], P(('gx', 'gy')), may hold values from 0.004 to 0.1
- tile_ids: int32 [1024], P(('gx', 'gy')), may hold values from -1 to 1023, as said below
- neighbors: int32 [1024, 4], P(('gx', 'gy')), may hold values from -1 to 1023, as said below
- moves: int32 [32, 2, 8, 2], P(('gx', 'gy')), may hold values from -1 to 1023, as said below
Outputs:
- new_depth: float32 [1024, 128, 128], P(('gx', 'gy'))
- new_discharge: float32 [1024, 2, 128, 128], P(('gx', 'gy'))
The draws below stay inside these ranges and needn't reach their ends.
Inputs may be any that keep to these rules, and one draw needn't show every extreme that they name: `tile_ids`: each owner's wet tiles after the moves fill its first slots: those that stayed, in curve order, then those arrived from lower gy, then those arrived from higher gy; an empty slot is -1. `neighbors`: links are symmetric and join only slots with tile_ids >= 0. The tile beside on side 0 or 1 is held by the same owner or by the owner at gx - 1 or gx + 1 respectively; on side 2 or 3 by the same owner or the owner at gy - 1 or gy + 1. At most 4 tiles of an owner have their side 0 (or side 1) neighbour on another owner, and at most 8 their side 2 (or side 3) neighbour; both bounds are reached on some owner. Entries are global slots, -1 if unused, used entries first. Leaving slots lie on the owner and hold no tile that stays; landing slots lie on the owner and are either left by a tile or hold no tile before the moves. The m-th tile leaving owner (a, b) toward higher gy is the m-th arriving at (a, b + 1) from lower gy, and likewise downward; owners at the ends of gy list nothing toward the outside. All 8 entries of a direction are used on some owners.
All inputs are finite; a program needn't handle non-finite values.
Results may differ from the reference program's by a relative error of at most 0.00002.
Values sent between devices are 32-bit elements; how exact they have to be, the bound alone decides.
A program may use at most 128 MiB of HBM per device.

```python
import math
import jax
import jax.numpy as jnp

TILE = 128
BLOCK_ROWS = 8
BLOCK_COLS = 4
STEPS = 4
SLOTS = 32
MOVERS = 8
OWNERS = 32
TILES = 1024
N_GX = 4
N_GY = 8


def layout(key):
    rows_all = BLOCK_ROWS * N_GX
    cols_all = BLOCK_COLS * N_GY
    key_level, key_roll = jax.random.split(jax.random.fold_in(key, 29))
    level = jax.random.randint(key_level, (N_GX, N_GY), 30, 96)
    roll = jax.random.randint(key_roll, (rows_all, cols_all), 0, 100)
    cutoff = jnp.repeat(jnp.repeat(level, BLOCK_ROWS, axis=0), BLOCK_COLS, axis=1)
    row_idx = jnp.arange(rows_all)[:, None]
    col_idx = jnp.arange(cols_all)[None, :]
    wet = (roll < cutoff) | (row_idx == BLOCK_ROWS - 1) | (row_idx == BLOCK_ROWS)
    wet = wet | (col_idx == BLOCK_COLS - 1) | (col_idx == BLOCK_COLS)

    def to_blocks(plane):
        return plane.reshape(N_GX, BLOCK_ROWS, N_GY, BLOCK_COLS).transpose(0, 2, 1, 3).reshape(N_GX, N_GY, SLOTS)

    def from_blocks(blocks):
        return blocks.reshape(N_GX, N_GY, BLOCK_ROWS, BLOCK_COLS).transpose(0, 2, 1, 3).reshape(rows_all, cols_all)
    local_row = jnp.arange(BLOCK_ROWS)[:, None]
    local_col = jnp.arange(BLOCK_COLS)[None, :]
    curve = (local_row * BLOCK_COLS + jnp.where(local_row % 2 == 0, local_col, BLOCK_COLS - 1 - local_col)).reshape(-1)
    earlier = curve[None, :] < curve[:, None]
    flat_col = jnp.arange(SLOTS) % BLOCK_COLS
    flat_row = jnp.arange(SLOTS) // BLOCK_COLS
    owner_col = jnp.arange(N_GY)[None, :, None]
    wet_blocks = to_blocks(wet)
    from_low = wet_blocks & (flat_col == 0)[None, None, :] & (owner_col >= 1)
    from_high = wet_blocks & (flat_col == BLOCK_COLS - 1)[None, None, :] & (owner_col <= N_GY - 2)
    stay = wet_blocks & ~from_low & ~from_high
    rank = jnp.sum(stay[:, :, None, :] & earlier[None, None], axis=-1).astype(jnp.int32)
    count_stay = jnp.sum(stay.astype(jnp.int32), -1)
    low_col = from_low.reshape(N_GX, N_GY, BLOCK_ROWS, BLOCK_COLS)[..., 0]
    high_col = from_high.reshape(N_GX, N_GY, BLOCK_ROWS, BLOCK_COLS)[..., BLOCK_COLS - 1]
    order_low = jnp.cumsum(low_col.astype(jnp.int32), -1) - 1
    order_high = jnp.cumsum(high_col.astype(jnp.int32), -1) - 1
    count_low = jnp.sum(low_col.astype(jnp.int32), -1)
    count_high = jnp.sum(high_col.astype(jnp.int32), -1)
    local_slot = jnp.where(stay, rank, jnp.where(from_low, count_stay[..., None] + order_low[..., flat_row], count_stay[..., None] + count_low[..., None] + order_high[..., flat_row]))
    owner = (jnp.arange(N_GX)[:, None] * N_GY + jnp.arange(N_GY)[None, :]).astype(jnp.int32)
    post = jnp.where(wet_blocks, owner[:, :, None] * SLOTS + local_slot, -1).astype(jnp.int32)
    post_grid = from_blocks(post)
    ids_grid = (row_idx * cols_all + col_idx).astype(jnp.int32)
    target = jnp.where(wet, post_grid, TILES).reshape(-1).astype(jnp.int32)
    tile_ids = jnp.full((TILES,), -1, jnp.int32).at[target].set(ids_grid.reshape(-1), mode='drop')
    padded = jnp.pad(post_grid, 1, constant_values=-1)
    sides = jnp.stack([padded[:-2, 1:-1], padded[2:, 1:-1], padded[1:-1, :-2], padded[1:-1, 2:]], -1).reshape(-1, 4)
    neighbors = jnp.full((TILES, 4), -1, jnp.int32).at[target].set(sides.astype(jnp.int32), mode='drop')
    entry = jnp.arange(MOVERS)[None, None, :]
    base = owner[..., None] * SLOTS + count_stay[..., None]
    arrive_low = jnp.where(entry < count_low[..., None], base + entry, -1)
    arrive_high = jnp.where(entry < count_high[..., None], base + count_low[..., None] + entry, -1)
    zero_col = jnp.zeros((N_GX, 1), jnp.int32)
    count_down = jnp.concatenate([zero_col, count_high[:, :-1]], 1)
    count_up = jnp.concatenate([count_low[:, 1:], zero_col], 1)
    leave_down = jnp.where(entry < count_down[..., None], base + entry, -1)
    leave_up = jnp.where(entry < count_up[..., None], base + count_down[..., None] + entry, -1)
    way_down = jnp.stack([leave_down, arrive_low], -1)
    way_up = jnp.stack([leave_up, arrive_high], -1)
    moves = jnp.stack([way_down, way_up], 2).reshape(OWNERS, 2, MOVERS, 2).astype(jnp.int32)
    return (tile_ids, neighbors, moves)


def draw_tile_ids(key, part):
    return layout(key)[0]


def draw_neighbors(key, part):
    return layout(key)[1]


def draw_moves(key, part):
    return layout(key)[2]


def draw_bed(key, part):
    rough = 0.3 * jax.random.normal(jax.random.fold_in(key, 5), (TILES, TILE, TILE), jnp.float32)
    return jnp.clip(rough, -1.5, 2.5)


def shard_levels(rng, extent, shards, smallest, largest):
    def one(position, parts):
        draws = jax.random.uniform(jax.random.fold_in(jax.random.fold_in(rng, 6), position), (parts,), jnp.float32, smallest / len(shards), largest / len(shards))
        return jnp.repeat(jnp.exp(draws), extent[position] // parts).reshape((-1,) + (1,) * (len(extent) - position - 1))

    gain = one(*shards[0])
    for cut in shards[1:]:
        gain = gain * one(*cut)
    return gain


def gaussian(rng, shape, spread, most, cuts=(), kind=jnp.bfloat16):
    values = spread * jax.random.normal(rng, shape, jnp.float32)
    if cuts:
        values = values * shard_levels(rng, shape, cuts, -0.22, 0.18)
    return jnp.clip(values, -most, most).astype(kind)


def setup_inputs(seed: int = 0) -> dict:
    arg_keys = jax.random.split(jax.random.key(seed), 8)
    depth = jnp.clip(0.1 + 1.9 * jax.random.uniform(arg_keys[0], (TILES, TILE, TILE), jnp.float32) ** shard_levels(arg_keys[0], (TILES, TILE, TILE), ((0, 32),), -0.2, 0.2), 0.1, 2.0)
    discharge = gaussian(arg_keys[1], (TILES, 2, TILE, TILE), 0.5, 3.0, ((0, 32),), jnp.float32)
    bed = draw_bed(jax.random.fold_in(arg_keys[7], 71), 0)
    friction = jnp.clip(jnp.exp(math.log(0.1) - 3.218876 * jax.random.uniform(arg_keys[3], (TILES, TILE, TILE), jnp.float32) ** shard_levels(arg_keys[3], (TILES, TILE, TILE), ((0, 32),), -0.2, 0.2)), 0.004, 0.1)
    tile_ids = draw_tile_ids(jax.random.fold_in(arg_keys[7], 71), 0)
    neighbors = draw_neighbors(jax.random.fold_in(arg_keys[7], 71), 0)
    moves = draw_moves(jax.random.fold_in(arg_keys[7], 71), 0)
    return {"depth": depth, "discharge": discharge, "bed": bed, "friction": friction, "tile_ids": tile_ids, "neighbors": neighbors, "moves": moves}


gravity = 9.81
step_time = 0.25
spacing = 2.0
min_depth = 0.15


def face_flux(flow, h_lo, h_hi, z_lo, z_hi, n_lo, n_hi):
    depth_face = jnp.maximum(0.5 * (h_lo + h_hi), min_depth)
    drive = flow - (gravity * step_time / spacing) * depth_face * ((h_hi + z_hi) - (h_lo + z_lo))
    drag = 1.0 + gravity * step_time * 0.5 * (n_lo + n_hi) * jnp.abs(flow) * jnp.exp(-(7.0 / 3.0) * jnp.log(depth_face))
    return drive / drag


def edge_take(rows, link):
    got = jnp.take(rows, jnp.maximum(link, 0).astype(jnp.int32), axis=0)
    return jnp.where((link >= 0)[:, None], got, 0.0)


def advance(h, qx, qy, z, fr, links):
    h_hi = jnp.concatenate([h[:, 1:, :], edge_take(h[:, 0, :], links[:, 1])[:, None, :]], 1)
    z_hi = jnp.concatenate([z[:, 1:, :], edge_take(z[:, 0, :], links[:, 1])[:, None, :]], 1)
    n_hi = jnp.concatenate([fr[:, 1:, :], edge_take(fr[:, 0, :], links[:, 1])[:, None, :]], 1)
    inside_x = jnp.arange(TILE)[None, :, None] < TILE - 1
    qx_new = jnp.where(inside_x | (links[:, 1] >= 0)[:, None, None], face_flux(qx, h, h_hi, z, z_hi, fr, n_hi), 0.0)
    h_rt = jnp.concatenate([h[:, :, 1:], edge_take(h[:, :, 0], links[:, 3])[:, :, None]], 2)
    z_rt = jnp.concatenate([z[:, :, 1:], edge_take(z[:, :, 0], links[:, 3])[:, :, None]], 2)
    n_rt = jnp.concatenate([fr[:, :, 1:], edge_take(fr[:, :, 0], links[:, 3])[:, :, None]], 2)
    inside_y = jnp.arange(TILE)[None, None, :] < TILE - 1
    qy_new = jnp.where(inside_y | (links[:, 3] >= 0)[:, None, None], face_flux(qy, h, h_rt, z, z_rt, fr, n_rt), 0.0)
    in_x = jnp.concatenate([edge_take(qx_new[:, -1, :], links[:, 0])[:, None, :], qx_new[:, :-1, :]], 1)
    in_y = jnp.concatenate([edge_take(qy_new[:, :, -1], links[:, 2])[:, :, None], qy_new[:, :, :-1]], 2)
    h_new = h + (step_time / spacing) * ((in_x - qx_new) + (in_y - qy_new))
    return h_new, qx_new, qy_new


def reference(depth, discharge, bed, friction, tile_ids, neighbors, moves):
    grid = moves.reshape(N_GX, N_GY, 2, MOVERS, 2)
    source = jnp.concatenate([grid[:, :-1, 1, :, 0].reshape(-1), grid[:, 1:, 0, :, 0].reshape(-1)]).astype(jnp.int32)
    target = jnp.concatenate([grid[:, 1:, 0, :, 1].reshape(-1), grid[:, :-1, 1, :, 1].reshape(-1)]).astype(jnp.int32)
    valid = source >= 0
    source_at = jnp.where(valid, source, TILES).astype(jnp.int32)
    target_at = jnp.where(valid, target, TILES).astype(jnp.int32)
    leaving = jnp.zeros((TILES,), bool).at[source_at].set(True, mode="drop")
    pick = jnp.maximum(source, 0).astype(jnp.int32)

    def settle(field):
        shape = (-1,) + (1,) * (field.ndim - 1)
        kept = jnp.where(leaving.reshape(shape), 0.0, field)
        return kept.at[target_at].set(jnp.take(field, pick, axis=0), mode="drop")

    h = settle(depth)
    flows = settle(discharge)
    z = settle(bed)
    fr = settle(friction)
    qx = flows[:, 0]
    qy = flows[:, 1]
    for turn in range(STEPS):
        h, qx, qy = advance(h, qx, qy, z, fr, neighbors)
    live = (tile_ids >= 0)[:, None, None]
    new_depth = jnp.where(live, h, 0.0)
    new_discharge = jnp.stack([jnp.where(live, qx, 0.0), jnp.where(live, qy, 0.0)], 1)
    return new_depth, new_discharge
```

```python
import functools

import jax
import jax.numpy as jnp
from jax import lax
from jax.experimental import pallas as pl
from jax.experimental.pallas import tpu as pltpu
from jax.sharding import PartitionSpec as P

BLOCK_ROWS = 8
BLOCK_COLS = 4
STEPS = 4

gravity = 9.81
step_time = 0.25
spacing = 2.0
min_depth = 0.15

F32 = jnp.float32
COUNTS = (BLOCK_COLS, BLOCK_COLS, BLOCK_ROWS, BLOCK_ROWS)
OPPOSITE = (1, 0, 3, 2)


def neighbour(block, axis, shift):
    count = lax.axis_size(axis)
    route = [(i + shift, i) for i in range(count) if 0 <= i + shift < count]
    return lax.ppermute(block, axis, route)


def face(q, depth_sum, rise, rough):
    d = jnp.maximum(0.5 * depth_sum, min_depth)
    drive = q - (gravity * step_time / spacing) * d * rise
    power = jnp.exp2(-(7.0 / 3.0) * jnp.log2(d))
    return drive / (1.0 + (gravity * step_time * 0.5) * rough * jnp.abs(q) * power)


def eye_of(tile):
    return lax.broadcasted_iota(jnp.int32, (tile, tile), 0) == lax.broadcasted_iota(
        jnp.int32, (tile, tile), 1
    )


def as_row(column, eye):
    return jnp.sum(jnp.where(eye, column, 0.0), 0, keepdims=True)


def as_column(row, eye):
    return jnp.sum(jnp.where(eye, row, 0.0), 1, keepdims=True)


def store_edges(ref, at, slot, x, eye):
    tile = x.shape[0]
    ref[at, pl.ds(slot, 1), :] = x[:1]
    ref[at + 1, pl.ds(slot, 1), :] = x[tile - 1 :]
    ref[at + 2, pl.ds(slot, 1), :] = as_row(x[:, :1], eye)
    ref[at + 3, pl.ds(slot, 1), :] = as_row(x[:, tile - 1 :], eye)


def fill_sends(pick_ref, edge_ref, send_refs, kinds):
    for side in range(4):
        for m in range(COUNTS[side]):
            slot = pick_ref[side, m]
            for j, kind in enumerate(kinds[side]):
                send_refs[side][j, m : m + 1, :] = edge_ref[kind, pl.ds(slot, 1), :]


FIRST_KINDS = ((0, 4, 8), (1, 5, 9, 12), (2, 6, 10), (3, 7, 11, 13))
LATER_KINDS = ((0,), (1,), (2,), (3,))


def bundle_kernel(down, up, *refs):
    ins, outs = refs[:8], refs[8:]
    for way in range(2):
        h, q, z, n = ins[4 * way : 4 * way + 4]
        out = outs[way]
        out[0, 0] = h[0]
        out[0, 1] = q[0, 0]
        out[0, 2] = q[0, 1]
        out[0, 3] = z[0]
        out[0, 4] = n[0]


def bundle(down, up, depth, discharge, bed, friction):
    tile = depth.shape[1]
    movers = down.shape[0]

    def one(which):
        return pl.BlockSpec((1, tile, tile), lambda m, d, u: ((d, u)[which][m], 0, 0))

    def two(which):
        return pl.BlockSpec((1, 2, tile, tile), lambda m, d, u: ((d, u)[which][m], 0, 0, 0))

    out = pl.BlockSpec((1, 5, tile, tile), lambda m, d, u: (m, 0, 0, 0))
    shape = jax.ShapeDtypeStruct((movers, 5, tile, tile), F32)
    return pl.pallas_call(
        bundle_kernel,
        grid_spec=pltpu.PrefetchScalarGridSpec(
            num_scalar_prefetch=2,
            grid=(movers,),
            in_specs=[one(0), two(0), one(0), one(0), one(1), two(1), one(1), one(1)],
            out_specs=[out, out],
        ),
        out_shape=[shape, shape],
        name="bundle",
    )(down, up, depth, discharge, bed, friction, depth, discharge, bed, friction)


def settle_kernel(mode, own, low, high, pick, *refs):
    h, q, z, n, lo, hi, ho, qo, zo, no, edges, s0, s1, s2, s3 = refs
    slot = pl.program_id(0)
    kind = mode[slot]

    @pl.when(kind == 0)
    def _():
        ho[...] = h[...]
        qo[...] = q[...]
        zo[...] = z[...]
        no[...] = n[...]

    def take(src):
        ho[0] = src[0, 0]
        qo[0, 0] = src[0, 1]
        qo[0, 1] = src[0, 2]
        zo[0] = src[0, 3]
        no[0] = src[0, 4]

    pl.when(kind == 1)(lambda: take(lo))
    pl.when(kind == 2)(lambda: take(hi))

    @pl.when(kind == 3)
    def _():
        for ref in (ho, qo, zo, no):
            ref[...] = jnp.zeros_like(ref)

    tile = h.shape[1]
    eye = eye_of(tile)
    store_edges(edges, 0, slot, ho[0], eye)
    store_edges(edges, 4, slot, zo[0], eye)
    store_edges(edges, 8, slot, no[0], eye)
    edges[12, pl.ds(slot, 1), :] = qo[0, 0, tile - 1 :, :]
    edges[13, pl.ds(slot, 1), :] = as_row(qo[0, 1][:, tile - 1 :], eye)

    @pl.when(slot == pl.num_programs(0) - 1)
    def _():
        fill_sends(pick, edges, (s0, s1, s2, s3), FIRST_KINDS)


def whole(shape):
    return pl.BlockSpec(shape, lambda *_: (0,) * len(shape))


def settle(mode, own, low, high, pick, depth, discharge, bed, friction, got_low, got_high):
    slots, tile = depth.shape[:2]
    one = pl.BlockSpec((1, tile, tile), lambda s, m, o, l, h, p: (o[s], 0, 0))
    two = pl.BlockSpec((1, 2, tile, tile), lambda s, m, o, l, h, p: (o[s], 0, 0, 0))
    lo = pl.BlockSpec((1, 5, tile, tile), lambda s, m, o, l, h, p: (l[s], 0, 0, 0))
    hi = pl.BlockSpec((1, 5, tile, tile), lambda s, m, o, l, h, p: (h[s], 0, 0, 0))
    out1 = pl.BlockSpec((1, tile, tile), lambda s, *_: (s, 0, 0))
    out2 = pl.BlockSpec((1, 2, tile, tile), lambda s, *_: (s, 0, 0, 0))
    sends = [(len(k), c, tile) for k, c in zip(FIRST_KINDS, COUNTS)]
    small = [(14, slots, tile)] + sends
    return pl.pallas_call(
        settle_kernel,
        grid_spec=pltpu.PrefetchScalarGridSpec(
            num_scalar_prefetch=5,
            grid=(slots,),
            in_specs=[one, two, one, one, lo, hi],
            out_specs=[out1, out2, out1, out1] + [whole(s) for s in small],
        ),
        out_shape=[
            jax.ShapeDtypeStruct(x.shape, F32) for x in (depth, discharge, bed, friction)
        ]
        + [jax.ShapeDtypeStruct(s, F32) for s in small],
        name="settle",
    )(mode, own, low, high, pick, depth, discharge, bed, friction, got_low, got_high)


def edge_fluxes(first, link, edges, gots, static, halo, flux):
    slots = halo.shape[1]

    def gather(side, kind, j, at):
        got = gots[side]
        count = got.shape[1]

        def body(s, _):
            k = link[side, s]
            near = edges[kind, pl.ds(jnp.clip(k, 0, slots - 1), 1), :]
            far = got[j, pl.ds(jnp.clip(k - slots, 0, count - 1), 1), :]
            row = jnp.where(k >= slots, far, near)
            halo[at, pl.ds(s, 1), :] = jnp.where(k >= 0, row, 0.0)
            return 0

        lax.fori_loop(0, slots, body, 0, unroll=8)

    q_old, rise_z, rough = static
    for side in range(4):
        other = OPPOSITE[side]
        gather(side, other, 0, 0)
        if first:
            gather(side, 4 + other, 1, 1)
            gather(side, 8 + other, 2, 2)
            dz = halo[1] - edges[4 + side]
            rise_z[side] = dz if side % 2 else -dz
            rough[side] = halo[2] + edges[8 + side]
            if side % 2:
                q = edges[12 + side // 2]
            else:
                gather(side, 12 + side // 2, 3, 3)
                q = halo[3]
        else:
            q = q_old[side]
        own = edges[side]
        dh = halo[0] - own
        rise = (dh if side % 2 else -dh) + rise_z[side]
        flux[side] = face(q, halo[0] + own, rise, rough[side])


def step_kernel(first, last, link, pick, live, *refs):
    refs = list(refs)

    def pop(count):
        out, refs[:count] = refs[:count], []
        return out

    h_ref, q_ref, z_ref, n_ref, edges = pop(5)
    gots = pop(4)
    if first:
        walls = pop(1)[0]
    else:
        q_old, rise_in, rough_in, walls = pop(4)
    ho, qo = pop(2)
    if not last:
        edges_out, s0, s1, s2, s3, flux = pop(6)
        if first:
            rise_out, rough_out = pop(2)
    else:
        flux = pop(1)[0]
        if first:
            rise_out, rough_out = pop(2)
    halo = pop(1)[0]
    slot = pl.program_id(0)
    static = (None, rise_out, rough_out) if first else (q_old, rise_in, rough_in)

    @pl.when(slot == 0)
    def _():
        edge_fluxes(first, link, edges, gots, static, halo, flux)
        flux[...] = jnp.where(walls[...] >= 0, flux[...], 0.0)

    h, z, n = h_ref[0], z_ref[0], n_ref[0]
    tile = h.shape[0]
    eye = eye_of(tile)
    row_id = lax.broadcasted_iota(jnp.int32, (tile, tile), 0)
    col_id = lax.broadcasted_iota(jnp.int32, (tile, tile), 1)
    w = h + z

    def along(dim, q, index, in_edge, out_edge):
        nxt = functools.partial(pltpu.roll, shift=tile - 1, axis=dim)
        flow = face(q, h + nxt(h), nxt(w) - w, n + nxt(n))
        flow = jnp.where(index == tile - 1, out_edge, flow)
        inflow = jnp.where(index == 0, in_edge, pltpu.roll(flow, 1, dim))
        return flow, inflow

    def edge(side):
        return flux[side, pl.ds(slot, 1), :]

    qx, in_x = along(0, q_ref[0, 0], row_id, edge(0), edge(1))
    qy, in_y = along(
        1, q_ref[0, 1], col_id, as_column(edge(2), eye), as_column(edge(3), eye)
    )
    h = h + (step_time / spacing) * ((in_x - qx) + (in_y - qy))
    if last:
        keep = live[slot] >= 0
        h = jnp.where(keep, h, 0.0)
        qx = jnp.where(keep, qx, 0.0)
        qy = jnp.where(keep, qy, 0.0)
    ho[0] = h
    qo[0, 0] = qx
    qo[0, 1] = qy
    if not last:
        store_edges(edges_out, 0, slot, h, eye)

        @pl.when(slot == pl.num_programs(0) - 1)
        def _():
            fill_sends(pick, edges_out, (s0, s1, s2, s3), LATER_KINDS)


def step(first, last, link, pick, live, state, edges, gots, static, walls):
    h, q, z, n = state
    slots, tile = h.shape[:2]
    one = pl.BlockSpec((1, tile, tile), lambda s, *_: (s, 0, 0))
    two = pl.BlockSpec((1, 2, tile, tile), lambda s, *_: (s, 0, 0, 0))
    table = (4, slots, tile)
    smalls_in = [edges, *gots, *static, walls]
    out_small = []
    if not last:
        out_small += [table] + [(len(k), c, tile) for k, c in zip(LATER_KINDS, COUNTS)]
    out_small += [table]
    if first:
        out_small += [table, table]
    return pl.pallas_call(
        functools.partial(step_kernel, first, last),
        grid_spec=pltpu.PrefetchScalarGridSpec(
            num_scalar_prefetch=3,
            grid=(slots,),
            in_specs=[one, two, one, one] + [whole(x.shape) for x in smalls_in],
            out_specs=[one, two] + [whole(s) for s in out_small],
            scratch_shapes=[pltpu.VMEM((4, slots, tile), F32)],
        ),
        out_shape=[jax.ShapeDtypeStruct(h.shape, F32), jax.ShapeDtypeStruct(q.shape, F32)]
        + [jax.ShapeDtypeStruct(s, F32) for s in out_small],
        name="step",
    )(link, pick, live, h, q, z, n, *smalls_in)


def exchange(sends):
    return [
        neighbour(sends[1], "gx", -1),
        neighbour(sends[0], "gx", 1),
        neighbour(sends[3], "gy", -1),
        neighbour(sends[2], "gy", 1),
    ]


def shards(depth, discharge, bed, friction, tile_ids, neighbors, moves):
    slots, tile = depth.shape[:2]
    owner_id = lax.axis_index("gx") * lax.axis_size("gy") + lax.axis_index("gy")
    base = owner_id * slots
    plan = moves[0]
    slot_id = jnp.arange(slots)

    leave = jnp.where(plan[:, :, 0] >= 0, plan[:, :, 0] - base, slots)
    land = jnp.where(plan[:, :, 1] >= 0, plan[:, :, 1] - base, slots)
    chosen = jnp.minimum(leave, slots - 1)
    to_low, to_high = bundle(chosen[0], chosen[1], depth, discharge, bed, friction)
    from_low = neighbour(to_high, "gy", -1)
    from_high = neighbour(to_low, "gy", 1)

    left = jnp.any(slot_id[:, None, None] == leave[None], (1, 2))
    lands = slot_id[:, None, None] == land[None]
    arrive = jnp.any(lands, 2)
    movers = plan.shape[1]
    entry = jnp.sum(jnp.where(lands, jnp.arange(movers)[None, None], 0), 2)
    mode = jnp.where(arrive[:, 0], 1, jnp.where(arrive[:, 1], 2, jnp.where(left, 3, 0)))

    def carried(used, value):
        seen = jnp.max(
            jnp.where(used[None] & (slot_id[None] <= slot_id[:, None]), slot_id[None], -1), 1
        )
        return jnp.sum(jnp.where(seen[:, None] == slot_id[None], value[None], 0), 1)

    own = carried(mode == 0, slot_id)
    low = carried(arrive[:, 0], entry[:, 0])
    high = carried(arrive[:, 1], entry[:, 1])

    links = neighbors.T
    remote = (links >= 0) & (links // slots != owner_id)
    rank = jnp.sum(remote[:, None, :] & (links[:, None, :] < links[:, :, None]), 2)
    link = jnp.where(remote, slots + rank, jnp.where(links >= 0, links - base, -1))
    before = jnp.sum(remote[:, None, :] & (slot_id[None, None] < slot_id[None, :, None]), 2)
    hit = remote[:, None, :] & (before[:, None, :] == jnp.arange(BLOCK_ROWS)[None, :, None])
    pick = jnp.sum(jnp.where(hit, slot_id[None, None], 0), 2)
    walls = jnp.broadcast_to(links[:, :, None], (4, slots, tile))
    as_int = lambda *xs: [x.astype(jnp.int32) for x in xs]
    mode, own, low, high, link, pick = as_int(mode, own, low, high, link, pick)

    h, q, z, n, edges, *sends = settle(
        mode, own, low, high, pick, depth, discharge, bed, friction, from_low, from_high
    )
    static = ()
    for turn in range(STEPS):
        first, last = turn == 0, turn == STEPS - 1
        gots = exchange(sends)
        h, q, *rest = step(
            first, last, link, pick, tile_ids, (h, q, z, n), edges, gots, static, walls
        )
        if not last:
            edges, *sends = rest[:5]
            rest = rest[5:]
        static = (rest[0],) + (tuple(rest[1:3]) if first else static[1:])
    return h, q


def solution(mesh):
    return jax.shard_map(
        shards,
        mesh=mesh,
        in_specs=(
            P(("gx", "gy"), None, None),
            P(("gx", "gy"), None, None, None),
            P(("gx", "gy"), None, None),
            P(("gx", "gy"), None, None),
            P(("gx", "gy")),
            P(("gx", "gy"), None),
            P(("gx", "gy"), None, None, None),
        ),
        out_specs=(P(("gx", "gy"), None, None), P(("gx", "gy"), None, None, None)),
        check_vma=False,
    )
```

```python
import functools

import jax
import jax.numpy as jnp
from jax import lax
from jax.experimental import pallas as pl
from jax.experimental.pallas import tpu as pltpu
from jax.sharding import PartitionSpec as P

BLOCK_ROWS = 8
BLOCK_COLS = 4
STEPS = 4

gravity = 9.81
step_time = 0.25
spacing = 2.0
min_depth = 0.15

F32 = jnp.float32
COUNTS = (BLOCK_COLS, BLOCK_COLS, BLOCK_ROWS, BLOCK_ROWS)
OPPOSITE = (1, 0, 3, 2)


def neighbour(block, axis, shift):
    count = lax.axis_size(axis)
    route = [(i + shift, i) for i in range(count) if 0 <= i + shift < count]
    return lax.ppermute(block, axis, route)


def face(q, depth_sum, rise, rough):
    d = jnp.maximum(0.5 * depth_sum, min_depth)
    drive = q - (gravity * step_time / spacing) * d * rise
    power = jnp.exp2(-(7.0 / 3.0) * jnp.log2(d))
    drag = 1.0 + (gravity * step_time * 0.5) * rough * jnp.abs(q) * power
    guess = pl.reciprocal(drag, approx=True)
    return drive * (guess * (2.0 - drag * guess))


def store_edges(ref, slot, x):
    tile = x.shape[0]
    turned = x.T
    ref[0, pl.ds(slot, 1), :] = x[:1]
    ref[1, pl.ds(slot, 1), :] = x[tile - 1 :]
    ref[2, pl.ds(slot, 1), :] = turned[:1]
    ref[3, pl.ds(slot, 1), :] = turned[tile - 1 :]


def fill_sends(pick_ref, edge_ref, send_refs, kinds):
    for side in range(4):
        for m in range(COUNTS[side]):
            slot = pick_ref[side, m]
            for j, kind in enumerate(kinds[side]):
                send_refs[side][j, m : m + 1, :] = edge_ref[kind, pl.ds(slot, 1), :]


FIRST_KINDS = ((0, 4, 8), (1, 5, 9, 12), (2, 6, 10), (3, 7, 11, 13))
LATER_KINDS = ((0,), (1,), (2,), (3,))


def bundle_kernel(down, up, *refs):
    ins, outs = refs[:8], refs[8:]
    for way in range(2):
        h, q, z, n = ins[4 * way : 4 * way + 4]
        out = outs[way]
        out[0, 0] = h[0]
        out[0, 1] = q[0, 0]
        out[0, 2] = q[0, 1]
        out[0, 3] = z[0]
        out[0, 4] = n[0]


def bundle(down, up, depth, discharge, bed, friction):
    tile = depth.shape[1]
    movers = down.shape[0]

    def one(which):
        return pl.BlockSpec((1, tile, tile), lambda m, d, u: ((d, u)[which][m], 0, 0))

    def two(which):
        return pl.BlockSpec((1, 2, tile, tile), lambda m, d, u: ((d, u)[which][m], 0, 0, 0))

    out = pl.BlockSpec((1, 5, tile, tile), lambda m, d, u: (m, 0, 0, 0))
    shape = jax.ShapeDtypeStruct((movers, 5, tile, tile), F32)
    return pl.pallas_call(
        bundle_kernel,
        grid_spec=pltpu.PrefetchScalarGridSpec(
            num_scalar_prefetch=2,
            grid=(movers,),
            in_specs=[one(0), two(0), one(0), one(0), one(1), two(1), one(1), one(1)],
            out_specs=[out, out],
        ),
        out_shape=[shape, shape],
        name="bundle",
    )(down, up, depth, discharge, bed, friction, depth, discharge, bed, friction)


def settle_kernel(mode, own, low, high, pick, *refs):
    h, q, z, n, lo, hi, ho, qo, zo, no, edges, s0, s1, s2, s3 = refs
    slot = pl.program_id(0)
    kind = mode[slot]

    @pl.when(kind == 0)
    def _():
        ho[...] = h[...]
        qo[...] = q[...]
        zo[...] = z[...]
        no[...] = n[...]

    def take(src):
        ho[0] = src[0, 0]
        qo[0, 0] = src[0, 1]
        qo[0, 1] = src[0, 2]
        zo[0] = src[0, 3]
        no[0] = src[0, 4]

    pl.when(kind == 1)(lambda: take(lo))
    pl.when(kind == 2)(lambda: take(hi))

    @pl.when(kind == 3)
    def _():
        for ref in (ho, qo, zo, no):
            ref[...] = jnp.zeros_like(ref)

    tile = h.shape[1]
    lane = lax.broadcasted_iota(jnp.int32, (tile, tile), 1)
    square = ho[0]
    for at, x in ((1, zo[0]), (3, no[0]), (5, qo[0, 1])):
        square = jnp.where(
            (lane == at) | (lane == at + 1), pltpu.roll(x, at + 1, 1), square
        )
    square = square.T
    for kind, ref in ((0, ho), (4, zo), (8, no)):
        edges[kind, pl.ds(slot, 1), :] = ref[0, :1, :]
        edges[kind + 1, pl.ds(slot, 1), :] = ref[0, tile - 1 :, :]
    for kind, at in ((2, 0), (3, tile - 1), (6, 2), (7, 1), (10, 4), (11, 3), (13, 5)):
        edges[kind, pl.ds(slot, 1), :] = square[at : at + 1]
    edges[12, pl.ds(slot, 1), :] = qo[0, 0, tile - 1 :, :]

    @pl.when(slot == pl.num_programs(0) - 1)
    def _():
        fill_sends(pick, edges, (s0, s1, s2, s3), FIRST_KINDS)


def whole(shape):
    return pl.BlockSpec(shape, lambda *_: (0,) * len(shape))


def settle(mode, own, low, high, pick, depth, discharge, bed, friction, got_low, got_high):
    slots, tile = depth.shape[:2]
    one = pl.BlockSpec((1, tile, tile), lambda s, m, o, l, h, p: (o[s], 0, 0))
    two = pl.BlockSpec((1, 2, tile, tile), lambda s, m, o, l, h, p: (o[s], 0, 0, 0))
    lo = pl.BlockSpec((1, 5, tile, tile), lambda s, m, o, l, h, p: (l[s], 0, 0, 0))
    hi = pl.BlockSpec((1, 5, tile, tile), lambda s, m, o, l, h, p: (h[s], 0, 0, 0))
    out1 = pl.BlockSpec((1, tile, tile), lambda s, *_: (s, 0, 0))
    out2 = pl.BlockSpec((1, 2, tile, tile), lambda s, *_: (s, 0, 0, 0))
    sends = [(len(k), c, tile) for k, c in zip(FIRST_KINDS, COUNTS)]
    small = [(14, slots, tile)] + sends
    return pl.pallas_call(
        settle_kernel,
        grid_spec=pltpu.PrefetchScalarGridSpec(
            num_scalar_prefetch=5,
            grid=(slots,),
            in_specs=[one, two, one, one, lo, hi],
            out_specs=[out1, out2, out1, out1] + [whole(s) for s in small],
        ),
        out_shape=[
            jax.ShapeDtypeStruct(x.shape, F32) for x in (depth, discharge, bed, friction)
        ]
        + [jax.ShapeDtypeStruct(s, F32) for s in small],
        name="settle",
    )(mode, own, low, high, pick, depth, discharge, bed, friction, got_low, got_high)


def edge_fluxes(first, link, edges, gots, static, halo, flux):
    slots = halo.shape[1]

    def gather(side, kind, j, at):
        got = gots[side]
        count = got.shape[1]

        def body(s, _):
            k = link[side, s]
            near = edges[kind, pl.ds(jnp.clip(k, 0, slots - 1), 1), :]
            far = got[j, pl.ds(jnp.clip(k - slots, 0, count - 1), 1), :]
            row = jnp.where(k >= slots, far, near)
            halo[at, pl.ds(s, 1), :] = jnp.where(k >= 0, row, 0.0)
            return 0

        lax.fori_loop(0, slots, body, 0, unroll=8)

    q_old, rise_z, rough = static
    for side in range(4):
        other = OPPOSITE[side]
        gather(side, other, 0, 0)
        if first:
            gather(side, 4 + other, 1, 1)
            gather(side, 8 + other, 2, 2)
            dz = halo[1] - edges[4 + side]
            rise_z[side] = dz if side % 2 else -dz
            rough[side] = halo[2] + edges[8 + side]
            if side % 2:
                q = edges[12 + side // 2]
            else:
                gather(side, 12 + side // 2, 3, 3)
                q = halo[3]
        else:
            q = q_old[side]
        own = edges[side]
        dh = halo[0] - own
        rise = (dh if side % 2 else -dh) + rise_z[side]
        flux[side] = face(q, halo[0] + own, rise, rough[side])


def step_kernel(first, last, link, pick, live, *refs):
    refs = list(refs)

    def pop(count):
        out, refs[:count] = refs[:count], []
        return out

    h_ref, q_ref, z_ref, n_ref, edges = pop(5)
    gots = pop(4)
    if first:
        walls = pop(1)[0]
    else:
        q_old, rise_in, rough_in, walls = pop(4)
    ho, qo = pop(2)
    if not last:
        edges_out, s0, s1, s2, s3, flux = pop(6)
        if first:
            rise_out, rough_out = pop(2)
    else:
        flux = pop(1)[0]
        if first:
            rise_out, rough_out = pop(2)
    halo = pop(1)[0]
    turn = pl.program_id(0)
    static = (None, rise_out, rough_out) if first else (q_old, rise_in, rough_in)

    @pl.when(turn == 0)
    def _():
        edge_fluxes(first, link, edges, gots, static, halo, flux)
        flux[...] = jnp.where(walls[...] >= 0, flux[...], 0.0)

    group, tile = h_ref.shape[:2]
    row_id = lax.broadcasted_iota(jnp.int32, (tile, tile), 0)
    col_id = lax.broadcasted_iota(jnp.int32, (tile, tile), 1)

    for i in range(group):
        slot = turn * group + i
        h, z, n = h_ref[i], z_ref[i], n_ref[i]
        w = h + z

        def along(dim, q, index, in_edge, out_edge):
            nxt = functools.partial(pltpu.roll, shift=tile - 1, axis=dim)
            flow = face(q, h + nxt(h), nxt(w) - w, n + nxt(n))
            flow = jnp.where(index == tile - 1, out_edge, flow)
            inflow = jnp.where(index == 0, in_edge, pltpu.roll(flow, 1, dim))
            return flow, inflow

        def edge(side):
            return flux[side, pl.ds(slot, 1), :]

        columns = jnp.where(row_id == 0, edge(2), jnp.where(row_id == tile - 1, edge(3), 0.0)).T
        qx, in_x = along(0, q_ref[i, 0], row_id, edge(0), edge(1))
        qy, in_y = along(1, q_ref[i, 1], col_id, columns, columns)
        h = h + (step_time / spacing) * ((in_x - qx) + (in_y - qy))
        if last:
            keep = live[slot] >= 0
            h = jnp.where(keep, h, 0.0)
            qx = jnp.where(keep, qx, 0.0)
            qy = jnp.where(keep, qy, 0.0)
        ho[i] = h
        qo[i, 0] = qx
        qo[i, 1] = qy
        if not last:
            store_edges(edges_out, slot, h)

    if not last:

        @pl.when(turn == pl.num_programs(0) - 1)
        def _():
            fill_sends(pick, edges_out, (s0, s1, s2, s3), LATER_KINDS)


def step(first, last, link, pick, live, state, edges, gots, static, walls):
    h, q, z, n = state
    slots, tile = h.shape[:2]
    group = 4 if slots % 4 == 0 else 1
    one = pl.BlockSpec((group, tile, tile), lambda s, *_: (s, 0, 0))
    two = pl.BlockSpec((group, 2, tile, tile), lambda s, *_: (s, 0, 0, 0))
    table = (4, slots, tile)
    smalls_in = [edges, *gots, *static, walls]
    out_small = []
    if not last:
        out_small += [table] + [(len(k), c, tile) for k, c in zip(LATER_KINDS, COUNTS)]
    out_small += [table]
    if first:
        out_small += [table, table]
    return pl.pallas_call(
        functools.partial(step_kernel, first, last),
        grid_spec=pltpu.PrefetchScalarGridSpec(
            num_scalar_prefetch=3,
            grid=(slots // group,),
            in_specs=[one, two, one, one] + [whole(x.shape) for x in smalls_in],
            out_specs=[one, two] + [whole(s) for s in out_small],
            scratch_shapes=[pltpu.VMEM((4, slots, tile), F32)],
        ),
        out_shape=[jax.ShapeDtypeStruct(h.shape, F32), jax.ShapeDtypeStruct(q.shape, F32)]
        + [jax.ShapeDtypeStruct(s, F32) for s in out_small],
        name="step",
    )(link, pick, live, h, q, z, n, *smalls_in)


def exchange_kernel(extent, *refs):
    sends, gots, (sent, landed) = refs[:4], refs[4:8], refs[8:]
    at = {axis: lax.axis_index(axis) for axis in extent}
    sides = (("gx", -1), ("gx", 1), ("gy", -1), ("gy", 1))
    there = [{axis: at[axis] + by} for axis, by in sides]
    has = [at[axis] > 0 if by < 0 else at[axis] < extent[axis] - 1 for axis, by in sides]
    barrier = pltpu.get_barrier_semaphore()

    def copy(side):
        other = OPPOSITE[side]
        return pltpu.make_async_remote_copy(
            src_ref=sends[side],
            dst_ref=gots[other],
            send_sem=sent.at[side],
            recv_sem=landed.at[other],
            device_id=there[side],
            device_id_type=pl.DeviceIdType.MESH,
        )

    for side in range(4):

        @pl.when(has[side])
        def _():
            pl.semaphore_signal(
                barrier, inc=1, device_id=there[side], device_id_type=pl.DeviceIdType.MESH
            )

    pl.semaphore_wait(barrier, sum(x.astype(jnp.int32) for x in has))
    for side in range(4):
        pl.when(has[side])(lambda: copy(side).start())
    for side in range(4):

        @pl.when(has[side])
        def _():
            copy(side).wait_send()
            copy(OPPOSITE[side]).wait_recv()

        @pl.when(jnp.logical_not(has[side]))
        def _():
            gots[side][...] = jnp.zeros_like(gots[side])


def exchange(turn, sends):
    extent = {axis: lax.axis_size(axis) for axis in ("gx", "gy")}
    vmem = pl.BlockSpec(memory_space=pltpu.VMEM)
    return pl.pallas_call(
        functools.partial(exchange_kernel, extent),
        in_specs=[vmem] * 4,
        out_specs=[vmem] * 4,
        out_shape=[jax.ShapeDtypeStruct(sends[o].shape, F32) for o in OPPOSITE],
        scratch_shapes=[pltpu.SemaphoreType.DMA((4,)), pltpu.SemaphoreType.DMA((4,))],
        compiler_params=pltpu.CompilerParams(collective_id=turn, has_side_effects=True),
        name="exchange",
    )(*sends)


def shards(depth, discharge, bed, friction, tile_ids, neighbors, moves):
    slots, tile = depth.shape[:2]
    owner_id = lax.axis_index("gx") * lax.axis_size("gy") + lax.axis_index("gy")
    base = owner_id * slots
    plan = moves[0]
    slot_id = jnp.arange(slots)

    leave = jnp.where(plan[:, :, 0] >= 0, plan[:, :, 0] - base, slots)
    land = jnp.where(plan[:, :, 1] >= 0, plan[:, :, 1] - base, slots)
    chosen = jnp.minimum(leave, slots - 1)
    to_low, to_high = bundle(chosen[0], chosen[1], depth, discharge, bed, friction)
    from_low = neighbour(to_high, "gy", -1)
    from_high = neighbour(to_low, "gy", 1)

    left = jnp.any(slot_id[:, None, None] == leave[None], (1, 2))
    lands = slot_id[:, None, None] == land[None]
    arrive = jnp.any(lands, 2)
    movers = plan.shape[1]
    entry = jnp.sum(jnp.where(lands, jnp.arange(movers)[None, None], 0), 2)
    mode = jnp.where(arrive[:, 0], 1, jnp.where(arrive[:, 1], 2, jnp.where(left, 3, 0)))

    def carried(used, value):
        seen = jnp.max(
            jnp.where(used[None] & (slot_id[None] <= slot_id[:, None]), slot_id[None], -1), 1
        )
        return jnp.sum(jnp.where(seen[:, None] == slot_id[None], value[None], 0), 1)

    own = carried(mode == 0, slot_id)
    low = carried(arrive[:, 0], entry[:, 0])
    high = carried(arrive[:, 1], entry[:, 1])

    links = neighbors.T
    remote = (links >= 0) & (links // slots != owner_id)
    rank = jnp.sum(remote[:, None, :] & (links[:, None, :] < links[:, :, None]), 2)
    link = jnp.where(remote, slots + rank, jnp.where(links >= 0, links - base, -1))
    before = jnp.sum(remote[:, None, :] & (slot_id[None, None] < slot_id[None, :, None]), 2)
    hit = remote[:, None, :] & (before[:, None, :] == jnp.arange(BLOCK_ROWS)[None, :, None])
    pick = jnp.sum(jnp.where(hit, slot_id[None, None], 0), 2)
    walls = jnp.broadcast_to(links[:, :, None], (4, slots, tile))
    as_int = lambda *xs: [x.astype(jnp.int32) for x in xs]
    mode, own, low, high, link, pick = as_int(mode, own, low, high, link, pick)

    h, q, z, n, edges, *sends = settle(
        mode, own, low, high, pick, depth, discharge, bed, friction, from_low, from_high
    )
    static = ()
    for turn in range(STEPS):
        first, last = turn == 0, turn == STEPS - 1
        gots = exchange(turn, sends)
        h, q, *rest = step(
            first, last, link, pick, tile_ids, (h, q, z, n), edges, gots, static, walls
        )
        if not last:
            edges, *sends = rest[:5]
            rest = rest[5:]
        static = (rest[0],) + (tuple(rest[1:3]) if first else static[1:])
    return h, q


def solution(mesh):
    return jax.shard_map(
        shards,
        mesh=mesh,
        in_specs=(
            P(("gx", "gy"), None, None),
            P(("gx", "gy"), None, None, None),
            P(("gx", "gy"), None, None),
            P(("gx", "gy"), None, None),
            P(("gx", "gy")),
            P(("gx", "gy"), None),
            P(("gx", "gy"), None, None, None),
        ),
        out_specs=(P(("gx", "gy"), None, None), P(("gx", "gy"), None, None, None)),
        check_vma=False,
    )
```

```python
import functools

import jax
import jax.numpy as jnp
from jax import lax
from jax.experimental import pallas as pl
from jax.experimental.pallas import tpu as pltpu
from jax.sharding import PartitionSpec as P

BLOCK_ROWS = 8
BLOCK_COLS = 4
STEPS = 4

gravity = 9.81
step_time = 0.25
spacing = 2.0
min_depth = 0.15

F32 = jnp.float32
COUNTS = (BLOCK_COLS, BLOCK_COLS, BLOCK_ROWS, BLOCK_ROWS)
OPPOSITE = (1, 0, 3, 2)


def neighbour(block, axis, shift):
    count = lax.axis_size(axis)
    route = [(i + shift, i) for i in range(count) if 0 <= i + shift < count]
    return lax.ppermute(block, axis, route)


def face(q, depth_sum, rise, rough):
    d = jnp.maximum(0.5 * depth_sum, min_depth)
    drive = q - (gravity * step_time / spacing) * d * rise
    power = jnp.exp2(-(7.0 / 3.0) * jnp.log2(d))
    drag = 1.0 + (gravity * step_time * 0.5) * rough * jnp.abs(q) * power
    guess = pl.reciprocal(drag, approx=True)
    return drive * (guess * (2.0 - drag * guess))


def store_edges(ref, slot, x):
    tile = x.shape[0]
    turned = x.T
    ref[0, pl.ds(slot, 1), :] = x[:1]
    ref[1, pl.ds(slot, 1), :] = x[tile - 1 :]
    ref[2, pl.ds(slot, 1), :] = turned[:1]
    ref[3, pl.ds(slot, 1), :] = turned[tile - 1 :]


def fill_sends(pick_ref, edge_ref, send_refs, kinds):
    for side in range(4):
        for m in range(COUNTS[side]):
            slot = pick_ref[side, m]
            for j, kind in enumerate(kinds[side]):
                send_refs[side][j, m : m + 1, :] = edge_ref[kind, pl.ds(slot, 1), :]


FIRST_KINDS = ((0, 4, 8), (1, 5, 9, 12), (2, 6, 10), (3, 7, 11, 13))
LATER_KINDS = ((0,), (1,), (2,), (3,))


def bundle_kernel(down, up, *refs):
    ins, outs = refs[:8], refs[8:]
    for way in range(2):
        h, q, z, n = ins[4 * way : 4 * way + 4]
        out = outs[way]
        out[0, 0] = h[0]
        out[0, 1] = q[0, 0]
        out[0, 2] = q[0, 1]
        out[0, 3] = z[0]
        out[0, 4] = n[0]


def bundle(down, up, depth, discharge, bed, friction):
    tile = depth.shape[1]
    movers = down.shape[0]

    def one(which):
        return pl.BlockSpec((1, tile, tile), lambda m, d, u: ((d, u)[which][m], 0, 0))

    def two(which):
        return pl.BlockSpec((1, 2, tile, tile), lambda m, d, u: ((d, u)[which][m], 0, 0, 0))

    out = pl.BlockSpec((1, 5, tile, tile), lambda m, d, u: (m, 0, 0, 0))
    shape = jax.ShapeDtypeStruct((movers, 5, tile, tile), F32)
    return pl.pallas_call(
        bundle_kernel,
        grid_spec=pltpu.PrefetchScalarGridSpec(
            num_scalar_prefetch=2,
            grid=(movers,),
            in_specs=[one(0), two(0), one(0), one(0), one(1), two(1), one(1), one(1)],
            out_specs=[out, out],
        ),
        out_shape=[shape, shape],
        name="bundle",
    )(down, up, depth, discharge, bed, friction, depth, discharge, bed, friction)


def settle_kernel(group, mode, own, low, high, pick, *refs):
    fields, outs = refs[: 6 * group], refs[6 * group :]
    edges, sends = outs[4], outs[5:]
    turn = pl.program_id(0)
    for i in range(group):
        settle_one(i, turn * group + i, mode, *fields[6 * i : 6 * i + 6], *outs[:4])
    for i in range(group):
        settled_edges(i, turn * group + i, *outs[:5])

    @pl.when(turn == pl.num_programs(0) - 1)
    def _():
        fill_sends(pick, edges, sends, FIRST_KINDS)


def settle_one(i, slot, mode, h, q, z, n, lo, hi, ho, qo, zo, no):
    kind = mode[slot]

    @pl.when(kind == 0)
    def _():
        ho[i] = h[0]
        qo[i] = q[0]
        zo[i] = z[0]
        no[i] = n[0]

    def take(src):
        ho[i] = src[0, 0]
        qo[i, 0] = src[0, 1]
        qo[i, 1] = src[0, 2]
        zo[i] = src[0, 3]
        no[i] = src[0, 4]

    pl.when(kind == 1)(lambda: take(lo))
    pl.when(kind == 2)(lambda: take(hi))

    @pl.when(kind == 3)
    def _():
        for ref in (ho, qo, zo, no):
            ref[i] = jnp.zeros(ref.shape[1:], F32)


def settled_edges(i, slot, ho, qo, zo, no, edges):
    tile = ho.shape[1]
    lane = lax.broadcasted_iota(jnp.int32, (tile, tile), 1)
    square = ho[i]
    for at, x in ((1, zo[i]), (3, no[i]), (5, qo[i, 1])):
        square = jnp.where(
            (lane == at) | (lane == at + 1), pltpu.roll(x, at + 1, 1), square
        )
    square = square.T
    for kind, ref in ((0, ho), (4, zo), (8, no)):
        edges[kind, pl.ds(slot, 1), :] = ref[i, :1, :]
        edges[kind + 1, pl.ds(slot, 1), :] = ref[i, tile - 1 :, :]
    for kind, at in ((2, 0), (3, tile - 1), (6, 2), (7, 1), (10, 4), (11, 3), (13, 5)):
        edges[kind, pl.ds(slot, 1), :] = square[at : at + 1]
    edges[12, pl.ds(slot, 1), :] = qo[i, 0, tile - 1 :, :]


def whole(shape):
    return pl.BlockSpec(shape, lambda *_: (0,) * len(shape))


def group_of(slots, most):
    return most if slots % most == 0 else 1


def settle(group, mode, own, low, high, pick, depth, discharge, bed, friction, got_low, got_high):
    slots, tile = depth.shape[:2]

    def block(i, lead, table):
        rest = (0,) * (len(lead) + 2)
        return pl.BlockSpec(
            (1, *lead, tile, tile), lambda s, *tables: (tables[table][s * group + i], *rest)
        )

    ins = []
    for i in range(group):
        one, two = block(i, (), 1), block(i, (2,), 1)
        ins += [one, two, one, one, block(i, (5,), 2), block(i, (5,), 3)]
    out1 = pl.BlockSpec((group, tile, tile), lambda s, *_: (s, 0, 0))
    out2 = pl.BlockSpec((group, 2, tile, tile), lambda s, *_: (s, 0, 0, 0))
    sends = [(len(k), c, tile) for k, c in zip(FIRST_KINDS, COUNTS)]
    small = [(14, slots, tile)] + sends
    return pl.pallas_call(
        functools.partial(settle_kernel, group),
        grid_spec=pltpu.PrefetchScalarGridSpec(
            num_scalar_prefetch=5,
            grid=(slots // group,),
            in_specs=ins,
            out_specs=[out1, out2, out1, out1] + [whole(s) for s in small],
        ),
        out_shape=[
            jax.ShapeDtypeStruct(x.shape, F32) for x in (depth, discharge, bed, friction)
        ]
        + [jax.ShapeDtypeStruct(s, F32) for s in small],
        compiler_params=pltpu.CompilerParams(vmem_limit_bytes=32 * 2**20),
        name="settle",
    )(mode, own, low, high, pick, *[depth, discharge, bed, friction, got_low, got_high] * group)


def edge_fluxes(first, link, edges, gots, static, halo, flux):
    slots = halo.shape[1]

    def gather(side, kind, j, at):
        got = gots[side]
        count = got.shape[1]

        def body(s, _):
            k = link[side, s]
            near = edges[kind, pl.ds(jnp.clip(k, 0, slots - 1), 1), :]
            far = got[j, pl.ds(jnp.clip(k - slots, 0, count - 1), 1), :]
            row = jnp.where(k >= slots, far, near)
            halo[at, pl.ds(s, 1), :] = jnp.where(k >= 0, row, 0.0)
            return 0

        lax.fori_loop(0, slots, body, 0, unroll=8)

    q_old, rise_z, rough = static
    for side in range(4):
        other = OPPOSITE[side]
        gather(side, other, 0, 0)
        if first:
            gather(side, 4 + other, 1, 1)
            gather(side, 8 + other, 2, 2)
            dz = halo[1] - edges[4 + side]
            rise_z[side] = dz if side % 2 else -dz
            rough[side] = halo[2] + edges[8 + side]
            if side % 2:
                q = edges[12 + side // 2]
            else:
                gather(side, 12 + side // 2, 3, 3)
                q = halo[3]
        else:
            q = q_old[side]
        own = edges[side]
        dh = halo[0] - own
        rise = (dh if side % 2 else -dh) + rise_z[side]
        flux[side] = face(q, halo[0] + own, rise, rough[side])


def step_kernel(first, last, link, pick, live, *refs):
    refs = list(refs)

    def pop(count):
        out, refs[:count] = refs[:count], []
        return out

    h_ref, q_ref, z_ref, n_ref, edges = pop(5)
    gots = pop(4)
    if first:
        walls = pop(1)[0]
    else:
        q_old, rise_in, rough_in, walls = pop(4)
    ho, qo = pop(2)
    if not last:
        edges_out, s0, s1, s2, s3, flux = pop(6)
        if first:
            rise_out, rough_out = pop(2)
    else:
        flux = pop(1)[0]
        if first:
            rise_out, rough_out = pop(2)
    halo = pop(1)[0]
    turn = pl.program_id(0)
    static = (None, rise_out, rough_out) if first else (q_old, rise_in, rough_in)

    @pl.when(turn == 0)
    def _():
        edge_fluxes(first, link, edges, gots, static, halo, flux)
        flux[...] = jnp.where(walls[...] >= 0, flux[...], 0.0)

    group, tile = h_ref.shape[:2]
    row_id = lax.broadcasted_iota(jnp.int32, (tile, tile), 0)
    col_id = lax.broadcasted_iota(jnp.int32, (tile, tile), 1)

    for i in range(group):
        slot = turn * group + i
        h, z, n = h_ref[i], z_ref[i], n_ref[i]
        w = h + z

        def along(dim, q, index, in_edge, out_edge):
            nxt = functools.partial(pltpu.roll, shift=tile - 1, axis=dim)
            flow = face(q, h + nxt(h), nxt(w) - w, n + nxt(n))
            flow = jnp.where(index == tile - 1, out_edge, flow)
            inflow = jnp.where(index == 0, in_edge, pltpu.roll(flow, 1, dim))
            return flow, inflow

        def edge(side):
            return flux[side, pl.ds(slot, 1), :]

        columns = jnp.where(row_id == 0, edge(2), jnp.where(row_id == tile - 1, edge(3), 0.0)).T
        qx, in_x = along(0, q_ref[i, 0], row_id, edge(0), edge(1))
        qy, in_y = along(1, q_ref[i, 1], col_id, columns, columns)
        h = h + (step_time / spacing) * ((in_x - qx) + (in_y - qy))
        if last:
            keep = live[slot] >= 0
            h = jnp.where(keep, h, 0.0)
            qx = jnp.where(keep, qx, 0.0)
            qy = jnp.where(keep, qy, 0.0)
        ho[i] = h
        qo[i, 0] = qx
        qo[i, 1] = qy
        if not last:
            store_edges(edges_out, slot, h)

    if not last:

        @pl.when(turn == pl.num_programs(0) - 1)
        def _():
            fill_sends(pick, edges_out, (s0, s1, s2, s3), LATER_KINDS)


def step(first, last, link, pick, live, state, edges, gots, static, walls):
    h, q, z, n = state
    slots, tile = h.shape[:2]
    group = group_of(slots, 8)
    one = pl.BlockSpec((group, tile, tile), lambda s, *_: (s, 0, 0))
    two = pl.BlockSpec((group, 2, tile, tile), lambda s, *_: (s, 0, 0, 0))
    table = (4, slots, tile)
    smalls_in = [edges, *gots, *static, walls]
    out_small = []
    if not last:
        out_small += [table] + [(len(k), c, tile) for k, c in zip(LATER_KINDS, COUNTS)]
    out_small += [table]
    if first:
        out_small += [table, table]
    return pl.pallas_call(
        functools.partial(step_kernel, first, last),
        grid_spec=pltpu.PrefetchScalarGridSpec(
            num_scalar_prefetch=3,
            grid=(slots // group,),
            in_specs=[one, two, one, one] + [whole(x.shape) for x in smalls_in],
            out_specs=[one, two] + [whole(s) for s in out_small],
            scratch_shapes=[pltpu.VMEM((4, slots, tile), F32)],
        ),
        out_shape=[jax.ShapeDtypeStruct(h.shape, F32), jax.ShapeDtypeStruct(q.shape, F32)]
        + [jax.ShapeDtypeStruct(s, F32) for s in out_small],
        compiler_params=pltpu.CompilerParams(vmem_limit_bytes=32 * 2**20),
        name="step",
    )(link, pick, live, h, q, z, n, *smalls_in)


def exchange_kernel(extent, *refs):
    sends, gots, (sent, landed) = refs[:4], refs[4:8], refs[8:]
    at = {axis: lax.axis_index(axis) for axis in extent}
    sides = (("gx", -1), ("gx", 1), ("gy", -1), ("gy", 1))
    there = [{axis: at[axis] + by} for axis, by in sides]
    has = [at[axis] > 0 if by < 0 else at[axis] < extent[axis] - 1 for axis, by in sides]
    barrier = pltpu.get_barrier_semaphore()

    def copy(side):
        other = OPPOSITE[side]
        return pltpu.make_async_remote_copy(
            src_ref=sends[side],
            dst_ref=gots[other],
            send_sem=sent.at[side],
            recv_sem=landed.at[other],
            device_id=there[side],
            device_id_type=pl.DeviceIdType.MESH,
        )

    for side in range(4):

        @pl.when(has[side])
        def _():
            pl.semaphore_signal(
                barrier, inc=1, device_id=there[side], device_id_type=pl.DeviceIdType.MESH
            )

    pl.semaphore_wait(barrier, sum(x.astype(jnp.int32) for x in has))
    for side in range(4):
        pl.when(has[side])(lambda: copy(side).start())
    for side in range(4):

        @pl.when(has[side])
        def _():
            copy(side).wait_send()
            copy(OPPOSITE[side]).wait_recv()

        @pl.when(jnp.logical_not(has[side]))
        def _():
            gots[side][...] = jnp.zeros_like(gots[side])


def exchange(turn, sends):
    extent = {axis: lax.axis_size(axis) for axis in ("gx", "gy")}
    vmem = pl.BlockSpec(memory_space=pltpu.VMEM)
    return pl.pallas_call(
        functools.partial(exchange_kernel, extent),
        in_specs=[vmem] * 4,
        out_specs=[vmem] * 4,
        out_shape=[jax.ShapeDtypeStruct(sends[o].shape, F32) for o in OPPOSITE],
        scratch_shapes=[pltpu.SemaphoreType.DMA((4,)), pltpu.SemaphoreType.DMA((4,))],
        compiler_params=pltpu.CompilerParams(collective_id=turn, has_side_effects=True),
        name="exchange",
    )(*sends)


def shards(depth, discharge, bed, friction, tile_ids, neighbors, moves):
    slots, tile = depth.shape[:2]
    owner_id = lax.axis_index("gx") * lax.axis_size("gy") + lax.axis_index("gy")
    base = owner_id * slots
    plan = moves[0]
    slot_id = jnp.arange(slots)
    group = group_of(slots, 4)
    together = slot_id[None] % group == slot_id[:, None] % group
    earlier = together & (slot_id[None] <= slot_id[:, None])

    leave = jnp.where(plan[:, :, 0] >= 0, plan[:, :, 0] - base, slots)
    land = jnp.where(plan[:, :, 1] >= 0, plan[:, :, 1] - base, slots)
    chosen = jnp.minimum(leave, slots - 1)
    to_low, to_high = bundle(chosen[0], chosen[1], depth, discharge, bed, friction)
    from_low = neighbour(to_high, "gy", -1)
    from_high = neighbour(to_low, "gy", 1)

    left = jnp.any(slot_id[:, None, None] == leave[None], (1, 2))
    lands = slot_id[:, None, None] == land[None]
    arrive = jnp.any(lands, 2)
    movers = plan.shape[1]
    entry = jnp.sum(jnp.where(lands, jnp.arange(movers)[None, None], 0), 2)
    mode = jnp.where(arrive[:, 0], 1, jnp.where(arrive[:, 1], 2, jnp.where(left, 3, 0)))

    def carried(used, value):
        seen = jnp.max(
            jnp.where(used[None] & earlier, slot_id[None], -1), 1
        )
        return jnp.sum(jnp.where(seen[:, None] == slot_id[None], value[None], 0), 1)

    own = carried(mode == 0, slot_id)
    low = carried(arrive[:, 0], entry[:, 0])
    high = carried(arrive[:, 1], entry[:, 1])

    links = neighbors.T
    remote = (links >= 0) & (links // slots != owner_id)
    rank = jnp.sum(remote[:, None, :] & (links[:, None, :] < links[:, :, None]), 2)
    link = jnp.where(remote, slots + rank, jnp.where(links >= 0, links - base, -1))
    before = jnp.sum(remote[:, None, :] & (slot_id[None, None] < slot_id[None, :, None]), 2)
    hit = remote[:, None, :] & (before[:, None, :] == jnp.arange(BLOCK_ROWS)[None, :, None])
    pick = jnp.sum(jnp.where(hit, slot_id[None, None], 0), 2)
    walls = jnp.broadcast_to(links[:, :, None], (4, slots, tile))
    as_int = lambda *xs: [x.astype(jnp.int32) for x in xs]
    mode, own, low, high, link, pick = as_int(mode, own, low, high, link, pick)

    h, q, z, n, edges, *sends = settle(
        group, mode, own, low, high, pick, depth, discharge, bed, friction, from_low, from_high
    )
    static = ()
    for turn in range(STEPS):
        first, last = turn == 0, turn == STEPS - 1
        gots = exchange(turn, sends)
        h, q, *rest = step(
            first, last, link, pick, tile_ids, (h, q, z, n), edges, gots, static, walls
        )
        if not last:
            edges, *sends = rest[:5]
            rest = rest[5:]
        static = (rest[0],) + (tuple(rest[1:3]) if first else static[1:])
    return h, q


def solution(mesh):
    return jax.shard_map(
        shards,
        mesh=mesh,
        in_specs=(
            P(("gx", "gy"), None, None),
            P(("gx", "gy"), None, None, None),
            P(("gx", "gy"), None, None),
            P(("gx", "gy"), None, None),
            P(("gx", "gy")),
            P(("gx", "gy"), None),
            P(("gx", "gy"), None, None, None),
        ),
        out_specs=(P(("gx", "gy"), None, None), P(("gx", "gy"), None, None, None)),
        check_vma=False,
    )
```

```python
import functools

import jax
import jax.numpy as jnp
from jax import lax
from jax.experimental import pallas as pl
from jax.experimental.pallas import tpu as pltpu
from jax.sharding import PartitionSpec as P

BLOCK_ROWS = 8
BLOCK_COLS = 4
STEPS = 4

gravity = 9.81
step_time = 0.25
spacing = 2.0
min_depth = 0.15

F32 = jnp.float32
COUNTS = (BLOCK_COLS, BLOCK_COLS, BLOCK_ROWS, BLOCK_ROWS)
OPPOSITE = (1, 0, 3, 2)


def neighbour(block, axis, shift):
    count = lax.axis_size(axis)
    route = [(i + shift, i) for i in range(count) if 0 <= i + shift < count]
    return lax.ppermute(block, axis, route)


def face(q, depth_sum, rise, rough):
    d = jnp.maximum(0.5 * depth_sum, min_depth)
    drive = q - (gravity * step_time / spacing) * d * rise
    power = jnp.exp2(-(7.0 / 3.0) * jnp.log2(d))
    drag = 1.0 + (gravity * step_time * 0.5) * rough * jnp.abs(q) * power
    guess = pl.reciprocal(drag, approx=True)
    return drive * (guess * (2.0 - drag * guess))


def store_edges(ref, slot, x):
    tile = x.shape[0]
    turned = x.T
    ref[0, pl.ds(slot, 1), :] = x[:1]
    ref[1, pl.ds(slot, 1), :] = x[tile - 1 :]
    ref[2, pl.ds(slot, 1), :] = turned[:1]
    ref[3, pl.ds(slot, 1), :] = turned[tile - 1 :]


def fill_sends(pick_ref, edge_ref, send_refs, kinds):
    for side in range(4):
        for m in range(COUNTS[side]):
            slot = pick_ref[side, m]
            for j, kind in enumerate(kinds[side]):
                send_refs[side][j, m : m + 1, :] = edge_ref[kind, pl.ds(slot, 1), :]


FIRST_KINDS = ((0, 4, 8), (1, 5, 9, 12), (2, 6, 10), (3, 7, 11, 13))
LATER_KINDS = ((0,), (1,), (2,), (3,))


def bundle_kernel(down, up, *refs):
    ins, outs = refs[:8], refs[8:]
    for way in range(2):
        h, q, z, n = ins[4 * way : 4 * way + 4]
        out = outs[way]
        out[0, 0] = h[0]
        out[0, 1] = q[0, 0]
        out[0, 2] = q[0, 1]
        out[0, 3] = z[0]
        out[0, 4] = n[0]


def bundle(down, up, depth, discharge, bed, friction):
    tile = depth.shape[1]
    movers = down.shape[0]

    def one(which):
        return pl.BlockSpec((1, tile, tile), lambda m, d, u: ((d, u)[which][m], 0, 0))

    def two(which):
        return pl.BlockSpec((1, 2, tile, tile), lambda m, d, u: ((d, u)[which][m], 0, 0, 0))

    out = pl.BlockSpec((1, 5, tile, tile), lambda m, d, u: (m, 0, 0, 0))
    shape = jax.ShapeDtypeStruct((movers, 5, tile, tile), F32)
    return pl.pallas_call(
        bundle_kernel,
        grid_spec=pltpu.PrefetchScalarGridSpec(
            num_scalar_prefetch=2,
            grid=(movers,),
            in_specs=[one(0), two(0), one(0), one(0), one(1), two(1), one(1), one(1)],
            out_specs=[out, out],
        ),
        out_shape=[shape, shape],
        name="bundle",
    )(down, up, depth, discharge, bed, friction, depth, discharge, bed, friction)


def settle_kernel(group, mode, own, low, high, pick, *refs):
    fields, outs = refs[: 6 * group], refs[6 * group :]
    edges, sends = outs[4], outs[5:]
    turn = pl.program_id(0)
    for i in range(group):
        settle_one(i, turn * group + i, mode, *fields[6 * i : 6 * i + 6], *outs[:4])
    for i in range(group):
        settled_edges(i, turn * group + i, *outs[:5])

    @pl.when(turn == pl.num_programs(0) - 1)
    def _():
        fill_sends(pick, edges, sends, FIRST_KINDS)


def settle_one(i, slot, mode, h, q, z, n, lo, hi, ho, qo, zo, no):
    kind = mode[slot]

    @pl.when(kind == 0)
    def _():
        ho[i] = h[0]
        qo[i] = q[0]
        zo[i] = z[0]
        no[i] = n[0]

    def take(src):
        ho[i] = src[0, 0]
        qo[i, 0] = src[0, 1]
        qo[i, 1] = src[0, 2]
        zo[i] = src[0, 3]
        no[i] = src[0, 4]

    pl.when(kind == 1)(lambda: take(lo))
    pl.when(kind == 2)(lambda: take(hi))

    @pl.when(kind == 3)
    def _():
        for ref in (ho, qo, zo, no):
            ref[i] = jnp.zeros(ref.shape[1:], F32)


def settled_edges(i, slot, ho, qo, zo, no, edges):
    tile = ho.shape[1]
    lane = lax.broadcasted_iota(jnp.int32, (tile, tile), 1)
    square = ho[i]
    for at, x in ((1, zo[i]), (3, no[i]), (5, qo[i, 1])):
        square = jnp.where(
            (lane == at) | (lane == at + 1), pltpu.roll(x, at + 1, 1), square
        )
    square = square.T
    for kind, ref in ((0, ho), (4, zo), (8, no)):
        edges[kind, pl.ds(slot, 1), :] = ref[i, :1, :]
        edges[kind + 1, pl.ds(slot, 1), :] = ref[i, tile - 1 :, :]
    for kind, at in ((2, 0), (3, tile - 1), (6, 2), (7, 1), (10, 4), (11, 3), (13, 5)):
        edges[kind, pl.ds(slot, 1), :] = square[at : at + 1]
    edges[12, pl.ds(slot, 1), :] = qo[i, 0, tile - 1 :, :]


def whole(shape):
    return pl.BlockSpec(shape, lambda *_: (0,) * len(shape))


def group_of(slots, most):
    return most if slots % most == 0 else 1


def settle(group, mode, own, low, high, pick, depth, discharge, bed, friction, got_low, got_high):
    slots, tile = depth.shape[:2]

    def block(i, lead, table):
        rest = (0,) * (len(lead) + 2)
        return pl.BlockSpec(
            (1, *lead, tile, tile), lambda s, *tables: (tables[table][s * group + i], *rest)
        )

    ins = []
    for i in range(group):
        one, two = block(i, (), 1), block(i, (2,), 1)
        ins += [one, two, one, one, block(i, (5,), 2), block(i, (5,), 3)]
    out1 = pl.BlockSpec((group, tile, tile), lambda s, *_: (s, 0, 0))
    out2 = pl.BlockSpec((group, 2, tile, tile), lambda s, *_: (s, 0, 0, 0))
    sends = [(len(k), c, tile) for k, c in zip(FIRST_KINDS, COUNTS)]
    small = [(14, slots, tile)] + sends
    return pl.pallas_call(
        functools.partial(settle_kernel, group),
        grid_spec=pltpu.PrefetchScalarGridSpec(
            num_scalar_prefetch=5,
            grid=(slots // group,),
            in_specs=ins,
            out_specs=[out1, out2, out1, out1] + [whole(s) for s in small],
        ),
        out_shape=[
            jax.ShapeDtypeStruct(x.shape, F32) for x in (depth, discharge, bed, friction)
        ]
        + [jax.ShapeDtypeStruct(s, F32) for s in small],
        name="settle",
    )(mode, own, low, high, pick, *[depth, discharge, bed, friction, got_low, got_high] * group)


def edge_fluxes(first, link, edges, gots, static, halo, flux):
    slots = halo.shape[1]

    def gather(side, kind, j, at):
        got = gots[side]
        count = got.shape[1]

        def body(s, _):
            k = link[side, s]
            near = edges[kind, pl.ds(jnp.clip(k, 0, slots - 1), 1), :]
            far = got[j, pl.ds(jnp.clip(k - slots, 0, count - 1), 1), :]
            row = jnp.where(k >= slots, far, near)
            halo[at, pl.ds(s, 1), :] = jnp.where(k >= 0, row, 0.0)
            return 0

        lax.fori_loop(0, slots, body, 0, unroll=8)

    q_old, rise_z, rough = static
    for side in range(4):
        other = OPPOSITE[side]
        gather(side, other, 0, 0)
        if first:
            gather(side, 4 + other, 1, 1)
            gather(side, 8 + other, 2, 2)
            dz = halo[1] - edges[4 + side]
            rise_z[side] = dz if side % 2 else -dz
            rough[side] = halo[2] + edges[8 + side]
            if side % 2:
                q = edges[12 + side // 2]
            else:
                gather(side, 12 + side // 2, 3, 3)
                q = halo[3]
        else:
            q = q_old[side]
        own = edges[side]
        dh = halo[0] - own
        rise = (dh if side % 2 else -dh) + rise_z[side]
        flux[side] = face(q, halo[0] + own, rise, rough[side])


def step_kernel(first, last, link, pick, live, *refs):
    refs = list(refs)

    def pop(count):
        out, refs[:count] = refs[:count], []
        return out

    h_ref, q_ref, z_ref, n_ref, edges = pop(5)
    gots = pop(4)
    if first:
        walls = pop(1)[0]
    else:
        q_old, rise_in, rough_in, walls = pop(4)
    ho, qo = pop(2)
    if not last:
        edges_out, s0, s1, s2, s3, flux = pop(6)
        if first:
            rise_out, rough_out = pop(2)
    else:
        flux = pop(1)[0]
        if first:
            rise_out, rough_out = pop(2)
    halo = pop(1)[0]
    turn = pl.program_id(0)
    static = (None, rise_out, rough_out) if first else (q_old, rise_in, rough_in)

    @pl.when(turn == 0)
    def _():
        edge_fluxes(first, link, edges, gots, static, halo, flux)
        flux[...] = jnp.where(walls[...] >= 0, flux[...], 0.0)

    group, tile = h_ref.shape[:2]
    row_id = lax.broadcasted_iota(jnp.int32, (tile, tile), 0)
    col_id = lax.broadcasted_iota(jnp.int32, (tile, tile), 1)

    for i in range(group):
        slot = turn * group + i
        h, z, n = h_ref[i], z_ref[i], n_ref[i]
        w = h + z

        def along(dim, q, index, in_edge, out_edge):
            nxt = functools.partial(pltpu.roll, shift=tile - 1, axis=dim)
            flow = face(q, h + nxt(h), nxt(w) - w, n + nxt(n))
            flow = jnp.where(index == tile - 1, out_edge, flow)
            inflow = jnp.where(index == 0, in_edge, pltpu.roll(flow, 1, dim))
            return flow, inflow

        def edge(side):
            return flux[side, pl.ds(slot, 1), :]

        columns = jnp.where(row_id == 0, edge(2), jnp.where(row_id == tile - 1, edge(3), 0.0)).T
        qx, in_x = along(0, q_ref[i, 0], row_id, edge(0), edge(1))
        qy, in_y = along(1, q_ref[i, 1], col_id, columns, columns)
        h = h + (step_time / spacing) * ((in_x - qx) + (in_y - qy))
        if last:
            keep = live[slot] >= 0
            h = jnp.where(keep, h, 0.0)
            qx = jnp.where(keep, qx, 0.0)
            qy = jnp.where(keep, qy, 0.0)
        ho[i] = h
        qo[i, 0] = qx
        qo[i, 1] = qy
        if not last:
            store_edges(edges_out, slot, h)

    if not last:

        @pl.when(turn == pl.num_programs(0) - 1)
        def _():
            fill_sends(pick, edges_out, (s0, s1, s2, s3), LATER_KINDS)


def step(first, last, link, pick, live, state, edges, gots, static, walls):
    h, q, z, n = state
    slots, tile = h.shape[:2]
    group = group_of(slots, 8)
    one = pl.BlockSpec((group, tile, tile), lambda s, *_: (s, 0, 0))
    two = pl.BlockSpec((group, 2, tile, tile), lambda s, *_: (s, 0, 0, 0))
    table = (4, slots, tile)
    smalls_in = [edges, *gots, *static, walls]
    out_small = []
    if not last:
        out_small += [table] + [(len(k), c, tile) for k, c in zip(LATER_KINDS, COUNTS)]
    out_small += [table]
    if first:
        out_small += [table, table]
    return pl.pallas_call(
        functools.partial(step_kernel, first, last),
        grid_spec=pltpu.PrefetchScalarGridSpec(
            num_scalar_prefetch=3,
            grid=(slots // group,),
            in_specs=[one, two, one, one] + [whole(x.shape) for x in smalls_in],
            out_specs=[one, two] + [whole(s) for s in out_small],
            scratch_shapes=[pltpu.VMEM((4, slots, tile), F32)],
        ),
        out_shape=[jax.ShapeDtypeStruct(h.shape, F32), jax.ShapeDtypeStruct(q.shape, F32)]
        + [jax.ShapeDtypeStruct(s, F32) for s in out_small],
        name="step",
    )(link, pick, live, h, q, z, n, *smalls_in)


def exchange_kernel(extent, *refs):
    sends, gots, (sent, landed) = refs[:4], refs[4:8], refs[8:]
    at = {axis: lax.axis_index(axis) for axis in extent}
    sides = (("gx", -1), ("gx", 1), ("gy", -1), ("gy", 1))
    there = [{axis: at[axis] + by} for axis, by in sides]
    has = [at[axis] > 0 if by < 0 else at[axis] < extent[axis] - 1 for axis, by in sides]
    barrier = pltpu.get_barrier_semaphore()

    def copy(side):
        other = OPPOSITE[side]
        return pltpu.make_async_remote_copy(
            src_ref=sends[side],
            dst_ref=gots[other],
            send_sem=sent.at[side],
            recv_sem=landed.at[other],
            device_id=there[side],
            device_id_type=pl.DeviceIdType.MESH,
        )

    for side in range(4):

        @pl.when(has[side])
        def _():
            pl.semaphore_signal(
                barrier, inc=1, device_id=there[side], device_id_type=pl.DeviceIdType.MESH
            )

    pl.semaphore_wait(barrier, sum(x.astype(jnp.int32) for x in has))
    for side in range(4):
        pl.when(has[side])(lambda: copy(side).start())
    for side in range(4):

        @pl.when(has[side])
        def _():
            copy(side).wait_send()
            copy(OPPOSITE[side]).wait_recv()

        @pl.when(jnp.logical_not(has[side]))
        def _():
            gots[side][...] = jnp.zeros_like(gots[side])


def exchange(turn, sends):
    extent = {axis: lax.axis_size(axis) for axis in ("gx", "gy")}
    vmem = pl.BlockSpec(memory_space=pltpu.VMEM)
    return pl.pallas_call(
        functools.partial(exchange_kernel, extent),
        in_specs=[vmem] * 4,
        out_specs=[vmem] * 4,
        out_shape=[jax.ShapeDtypeStruct(sends[o].shape, F32) for o in OPPOSITE],
        scratch_shapes=[pltpu.SemaphoreType.DMA((4,)), pltpu.SemaphoreType.DMA((4,))],
        compiler_params=pltpu.CompilerParams(collective_id=turn, has_side_effects=True),
        name="exchange",
    )(*sends)


def shards(depth, discharge, bed, friction, tile_ids, neighbors, moves):
    slots, tile = depth.shape[:2]
    owner_id = lax.axis_index("gx") * lax.axis_size("gy") + lax.axis_index("gy")
    base = owner_id * slots
    plan = moves[0]
    slot_id = jnp.arange(slots)
    group = group_of(slots, 4)
    together = slot_id[None] % group == slot_id[:, None] % group
    earlier = together & (slot_id[None] <= slot_id[:, None])

    leave = jnp.where(plan[:, :, 0] >= 0, plan[:, :, 0] - base, slots)
    land = jnp.where(plan[:, :, 1] >= 0, plan[:, :, 1] - base, slots)
    chosen = jnp.minimum(leave, slots - 1)
    to_low, to_high = bundle(chosen[0], chosen[1], depth, discharge, bed, friction)
    from_low = neighbour(to_high, "gy", -1)
    from_high = neighbour(to_low, "gy", 1)

    left = jnp.any(slot_id[:, None, None] == leave[None], (1, 2))
    lands = slot_id[:, None, None] == land[None]
    arrive = jnp.any(lands, 2)
    movers = plan.shape[1]
    entry = jnp.sum(jnp.where(lands, jnp.arange(movers)[None, None], 0), 2)
    mode = jnp.where(arrive[:, 0], 1, jnp.where(arrive[:, 1], 2, jnp.where(left, 3, 0)))

    def carried(used, value):
        seen = jnp.max(
            jnp.where(used[None] & earlier, slot_id[None], -1), 1
        )
        return jnp.sum(jnp.where(seen[:, None] == slot_id[None], value[None], 0), 1)

    own = carried(mode == 0, slot_id)
    low = carried(arrive[:, 0], entry[:, 0])
    high = carried(arrive[:, 1], entry[:, 1])

    links = neighbors.T
    remote = (links >= 0) & (links // slots != owner_id)
    rank = jnp.sum(remote[:, None, :] & (links[:, None, :] < links[:, :, None]), 2)
    link = jnp.where(remote, slots + rank, jnp.where(links >= 0, links - base, -1))
    before = jnp.sum(remote[:, None, :] & (slot_id[None, None] < slot_id[None, :, None]), 2)
    hit = remote[:, None, :] & (before[:, None, :] == jnp.arange(BLOCK_ROWS)[None, :, None])
    pick = jnp.sum(jnp.where(hit, slot_id[None, None], 0), 2)
    walls = jnp.broadcast_to(links[:, :, None], (4, slots, tile))
    as_int = lambda *xs: [x.astype(jnp.int32) for x in xs]
    mode, own, low, high, link, pick = as_int(mode, own, low, high, link, pick)

    h, q, z, n, edges, *sends = settle(
        group, mode, own, low, high, pick, depth, discharge, bed, friction, from_low, from_high
    )
    static = ()
    for turn in range(STEPS):
        first, last = turn == 0, turn == STEPS - 1
        gots = exchange(turn, sends)
        h, q, *rest = step(
            first, last, link, pick, tile_ids, (h, q, z, n), edges, gots, static, walls
        )
        if not last:
            edges, *sends = rest[:5]
            rest = rest[5:]
        static = (rest[0],) + (tuple(rest[1:3]) if first else static[1:])
    return h, q


def solution(mesh):
    return jax.shard_map(
        shards,
        mesh=mesh,
        in_specs=(
            P(("gx", "gy"), None, None),
            P(("gx", "gy"), None, None, None),
            P(("gx", "gy"), None, None),
            P(("gx", "gy"), None, None),
            P(("gx", "gy")),
            P(("gx", "gy"), None),
            P(("gx", "gy"), None, None, None),
        ),
        out_specs=(P(("gx", "gy"), None, None), P(("gx", "gy"), None, None, None)),
        check_vma=False,
    )
```

```python
import functools

import jax
import jax.numpy as jnp
from jax import lax
from jax.experimental import pallas as pl
from jax.experimental.pallas import tpu as pltpu
from jax.sharding import PartitionSpec as P

BLOCK_ROWS = 8
BLOCK_COLS = 4
STEPS = 4

gravity = 9.81
step_time = 0.25
spacing = 2.0
min_depth = 0.15

F32 = jnp.float32
COUNTS = (BLOCK_COLS, BLOCK_COLS, BLOCK_ROWS, BLOCK_ROWS)
OPPOSITE = (1, 0, 3, 2)


def neighbour(block, axis, shift):
    count = lax.axis_size(axis)
    route = [(i + shift, i) for i in range(count) if 0 <= i + shift < count]
    return lax.ppermute(block, axis, route)


def face(q, depth_sum, rise, rough):
    d = jnp.maximum(0.5 * depth_sum, min_depth)
    drive = q - (gravity * step_time / spacing) * d * rise
    power = jnp.exp2(-(7.0 / 3.0) * jnp.log2(d))
    drag = 1.0 + (gravity * step_time * 0.5) * rough * jnp.abs(q) * power
    guess = pl.reciprocal(drag, approx=True)
    return drive * (guess * (2.0 - drag * guess))


def store_edges(ref, slot, x):
    tile = x.shape[0]
    turned = x.T
    ref[0, pl.ds(slot, 1), :] = x[:1]
    ref[1, pl.ds(slot, 1), :] = x[tile - 1 :]
    ref[2, pl.ds(slot, 1), :] = turned[:1]
    ref[3, pl.ds(slot, 1), :] = turned[tile - 1 :]


def fill_sends(pick_ref, edge_ref, send_refs, kinds):
    for side in range(4):
        for m in range(COUNTS[side]):
            slot = pick_ref[side, m]
            for j, kind in enumerate(kinds[side]):
                send_refs[side][j, m : m + 1, :] = edge_ref[kind, pl.ds(slot, 1), :]


FIRST_KINDS = ((0, 4, 8), (1, 5, 9, 12), (2, 6, 10), (3, 7, 11, 13))
LATER_KINDS = ((0,), (1,), (2,), (3,))


def bundle_kernel(group, down, up, *refs):
    ins, outs = refs[: 8 * group], refs[8 * group :]
    for i in range(group):
        for way in range(2):
            at = 8 * i + 4 * way
            h, q, z, n = ins[at : at + 4]
            out = outs[way]
            out[i, 0] = h[0]
            out[i, 1] = q[0, 0]
            out[i, 2] = q[0, 1]
            out[i, 3] = z[0]
            out[i, 4] = n[0]


def bundle(down, up, depth, discharge, bed, friction):
    tile = depth.shape[1]
    movers = down.shape[0]
    group = group_of(movers, 2)

    def one(i, way):
        return pl.BlockSpec(
            (1, tile, tile), lambda m, *tables: (tables[way][m * group + i], 0, 0)
        )

    def two(i, way):
        return pl.BlockSpec(
            (1, 2, tile, tile), lambda m, *tables: (tables[way][m * group + i], 0, 0, 0)
        )

    ins = []
    for i in range(group):
        for way in range(2):
            ins += [one(i, way), two(i, way), one(i, way), one(i, way)]
    out = pl.BlockSpec((group, 5, tile, tile), lambda m, *_: (m, 0, 0, 0))
    shape = jax.ShapeDtypeStruct((movers, 5, tile, tile), F32)
    return pl.pallas_call(
        functools.partial(bundle_kernel, group),
        grid_spec=pltpu.PrefetchScalarGridSpec(
            num_scalar_prefetch=2,
            grid=(movers // group,),
            in_specs=ins,
            out_specs=[out, out],
        ),
        out_shape=[shape, shape],
        name="bundle",
    )(down, up, *[depth, discharge, bed, friction] * (2 * group))


def settle_kernel(group, mode, own, low, high, pick, *refs):
    fields, outs = refs[: 6 * group], refs[6 * group :]
    edges, sends = outs[4], outs[5:]
    turn = pl.program_id(0)
    for i in range(group):
        settle_one(i, turn * group + i, mode, *fields[6 * i : 6 * i + 6], *outs[:4])
    for i in range(group):
        settled_edges(i, turn * group + i, *outs[:5])

    @pl.when(turn == pl.num_programs(0) - 1)
    def _():
        fill_sends(pick, edges, sends, FIRST_KINDS)


def settle_one(i, slot, mode, h, q, z, n, lo, hi, ho, qo, zo, no):
    kind = mode[slot]

    @pl.when(kind == 0)
    def _():
        ho[i] = h[0]
        qo[i] = q[0]
        zo[i] = z[0]
        no[i] = n[0]

    def take(src):
        ho[i] = src[0, 0]
        qo[i, 0] = src[0, 1]
        qo[i, 1] = src[0, 2]
        zo[i] = src[0, 3]
        no[i] = src[0, 4]

    pl.when(kind == 1)(lambda: take(lo))
    pl.when(kind == 2)(lambda: take(hi))

    @pl.when(kind == 3)
    def _():
        for ref in (ho, qo, zo, no):
            ref[i] = jnp.zeros(ref.shape[1:], F32)


def settled_edges(i, slot, ho, qo, zo, no, edges):
    tile = ho.shape[1]
    lane = lax.broadcasted_iota(jnp.int32, (tile, tile), 1)
    square = ho[i]
    for at, x in ((1, zo[i]), (3, no[i]), (5, qo[i, 1])):
        square = jnp.where(
            (lane == at) | (lane == at + 1), pltpu.roll(x, at + 1, 1), square
        )
    square = square.T
    for kind, ref in ((0, ho), (4, zo), (8, no)):
        edges[kind, pl.ds(slot, 1), :] = ref[i, :1, :]
        edges[kind + 1, pl.ds(slot, 1), :] = ref[i, tile - 1 :, :]
    for kind, at in ((2, 0), (3, tile - 1), (6, 2), (7, 1), (10, 4), (11, 3), (13, 5)):
        edges[kind, pl.ds(slot, 1), :] = square[at : at + 1]
    edges[12, pl.ds(slot, 1), :] = qo[i, 0, tile - 1 :, :]


def whole(shape):
    return pl.BlockSpec(shape, lambda *_: (0,) * len(shape))


def group_of(slots, most):
    return most if slots % most == 0 else 1


def settle(group, mode, own, low, high, pick, depth, discharge, bed, friction, got_low, got_high):
    slots, tile = depth.shape[:2]

    def block(i, lead, table):
        rest = (0,) * (len(lead) + 2)
        return pl.BlockSpec(
            (1, *lead, tile, tile), lambda s, *tables: (tables[table][s * group + i], *rest)
        )

    ins = []
    for i in range(group):
        one, two = block(i, (), 1), block(i, (2,), 1)
        ins += [one, two, one, one, block(i, (5,), 2), block(i, (5,), 3)]
    out1 = pl.BlockSpec((group, tile, tile), lambda s, *_: (s, 0, 0))
    out2 = pl.BlockSpec((group, 2, tile, tile), lambda s, *_: (s, 0, 0, 0))
    sends = [(len(k), c, tile) for k, c in zip(FIRST_KINDS, COUNTS)]
    small = [(14, slots, tile)] + sends
    return pl.pallas_call(
        functools.partial(settle_kernel, group),
        grid_spec=pltpu.PrefetchScalarGridSpec(
            num_scalar_prefetch=5,
            grid=(slots // group,),
            in_specs=ins,
            out_specs=[out1, out2, out1, out1] + [whole(s) for s in small],
        ),
        out_shape=[
            jax.ShapeDtypeStruct(x.shape, F32) for x in (depth, discharge, bed, friction)
        ]
        + [jax.ShapeDtypeStruct(s, F32) for s in small],
        name="settle",
    )(mode, own, low, high, pick, *[depth, discharge, bed, friction, got_low, got_high] * group)


def edge_fluxes(first, link, edges, gots, static, halo, flux):
    slots = halo.shape[1]

    def gather(side, kind, j, at):
        got = gots[side]
        count = got.shape[1]

        def body(s, _):
            k = link[side, s]
            near = edges[kind, pl.ds(jnp.clip(k, 0, slots - 1), 1), :]
            far = got[j, pl.ds(jnp.clip(k - slots, 0, count - 1), 1), :]
            row = jnp.where(k >= slots, far, near)
            halo[at, pl.ds(s, 1), :] = jnp.where(k >= 0, row, 0.0)
            return 0

        lax.fori_loop(0, slots, body, 0, unroll=8)

    q_old, rise_z, rough = static
    for side in range(4):
        other = OPPOSITE[side]
        gather(side, other, 0, 0)
        if first:
            gather(side, 4 + other, 1, 1)
            gather(side, 8 + other, 2, 2)
            dz = halo[1] - edges[4 + side]
            rise_z[side] = dz if side % 2 else -dz
            rough[side] = halo[2] + edges[8 + side]
            if side % 2:
                q = edges[12 + side // 2]
            else:
                gather(side, 12 + side // 2, 3, 3)
                q = halo[3]
        else:
            q = q_old[side]
        own = edges[side]
        dh = halo[0] - own
        rise = (dh if side % 2 else -dh) + rise_z[side]
        flux[side] = face(q, halo[0] + own, rise, rough[side])


def step_kernel(first, last, link, pick, live, *refs):
    refs = list(refs)

    def pop(count):
        out, refs[:count] = refs[:count], []
        return out

    h_ref, q_ref, z_ref, n_ref, edges = pop(5)
    gots = pop(4)
    if first:
        walls = pop(1)[0]
    else:
        q_old, rise_in, rough_in, walls = pop(4)
    ho, qo = pop(2)
    if not last:
        edges_out, s0, s1, s2, s3, flux = pop(6)
        if first:
            rise_out, rough_out = pop(2)
    else:
        flux = pop(1)[0]
        if first:
            rise_out, rough_out = pop(2)
    halo = pop(1)[0]
    turn = pl.program_id(0)
    static = (None, rise_out, rough_out) if first else (q_old, rise_in, rough_in)

    @pl.when(turn == 0)
    def _():
        edge_fluxes(first, link, edges, gots, static, halo, flux)
        flux[...] = jnp.where(walls[...] >= 0, flux[...], 0.0)

    group, tile = h_ref.shape[:2]
    row_id = lax.broadcasted_iota(jnp.int32, (tile, tile), 0)
    col_id = lax.broadcasted_iota(jnp.int32, (tile, tile), 1)

    for i in range(group):
        slot = turn * group + i
        h, z, n = h_ref[i], z_ref[i], n_ref[i]
        w = h + z

        def along(dim, q, index, in_edge, out_edge):
            nxt = functools.partial(pltpu.roll, shift=tile - 1, axis=dim)
            flow = face(q, h + nxt(h), nxt(w) - w, n + nxt(n))
            flow = jnp.where(index == tile - 1, out_edge, flow)
            inflow = jnp.where(index == 0, in_edge, pltpu.roll(flow, 1, dim))
            return flow, inflow

        def edge(side):
            return flux[side, pl.ds(slot, 1), :]

        columns = jnp.where(row_id == 0, edge(2), jnp.where(row_id == tile - 1, edge(3), 0.0)).T
        qx, in_x = along(0, q_ref[i, 0], row_id, edge(0), edge(1))
        qy, in_y = along(1, q_ref[i, 1], col_id, columns, columns)
        h = h + (step_time / spacing) * ((in_x - qx) + (in_y - qy))
        if last:
            keep = live[slot] >= 0
            h = jnp.where(keep, h, 0.0)
            qx = jnp.where(keep, qx, 0.0)
            qy = jnp.where(keep, qy, 0.0)
        ho[i] = h
        qo[i, 0] = qx
        qo[i, 1] = qy
        if not last:
            store_edges(edges_out, slot, h)

    if not last:

        @pl.when(turn == pl.num_programs(0) - 1)
        def _():
            fill_sends(pick, edges_out, (s0, s1, s2, s3), LATER_KINDS)


def step(first, last, link, pick, live, state, edges, gots, static, walls):
    h, q, z, n = state
    slots, tile = h.shape[:2]
    group = group_of(slots, 8)
    one = pl.BlockSpec((group, tile, tile), lambda s, *_: (s, 0, 0))
    two = pl.BlockSpec((group, 2, tile, tile), lambda s, *_: (s, 0, 0, 0))
    table = (4, slots, tile)
    smalls_in = [edges, *gots, *static, walls]
    out_small = []
    if not last:
        out_small += [table] + [(len(k), c, tile) for k, c in zip(LATER_KINDS, COUNTS)]
    out_small += [table]
    if first:
        out_small += [table, table]
    return pl.pallas_call(
        functools.partial(step_kernel, first, last),
        grid_spec=pltpu.PrefetchScalarGridSpec(
            num_scalar_prefetch=3,
            grid=(slots // group,),
            in_specs=[one, two, one, one] + [whole(x.shape) for x in smalls_in],
            out_specs=[one, two] + [whole(s) for s in out_small],
            scratch_shapes=[pltpu.VMEM((4, slots, tile), F32)],
        ),
        out_shape=[jax.ShapeDtypeStruct(h.shape, F32), jax.ShapeDtypeStruct(q.shape, F32)]
        + [jax.ShapeDtypeStruct(s, F32) for s in out_small],
        name="step",
    )(link, pick, live, h, q, z, n, *smalls_in)


def exchange_kernel(extent, *refs):
    sends, gots, (sent, landed) = refs[:4], refs[4:8], refs[8:]
    at = {axis: lax.axis_index(axis) for axis in extent}
    sides = (("gx", -1), ("gx", 1), ("gy", -1), ("gy", 1))
    there = [{axis: at[axis] + by} for axis, by in sides]
    has = [at[axis] > 0 if by < 0 else at[axis] < extent[axis] - 1 for axis, by in sides]
    barrier = pltpu.get_barrier_semaphore()

    def copy(side):
        other = OPPOSITE[side]
        return pltpu.make_async_remote_copy(
            src_ref=sends[side],
            dst_ref=gots[other],
            send_sem=sent.at[side],
            recv_sem=landed.at[other],
            device_id=there[side],
            device_id_type=pl.DeviceIdType.MESH,
        )

    for side in range(4):

        @pl.when(has[side])
        def _():
            pl.semaphore_signal(
                barrier, inc=1, device_id=there[side], device_id_type=pl.DeviceIdType.MESH
            )

    pl.semaphore_wait(barrier, sum(x.astype(jnp.int32) for x in has))
    for side in range(4):
        pl.when(has[side])(lambda: copy(side).start())
    for side in range(4):

        @pl.when(has[side])
        def _():
            copy(side).wait_send()
            copy(OPPOSITE[side]).wait_recv()

        @pl.when(jnp.logical_not(has[side]))
        def _():
            gots[side][...] = jnp.zeros_like(gots[side])


def exchange(turn, sends):
    extent = {axis: lax.axis_size(axis) for axis in ("gx", "gy")}
    vmem = pl.BlockSpec(memory_space=pltpu.VMEM)
    return pl.pallas_call(
        functools.partial(exchange_kernel, extent),
        in_specs=[vmem] * 4,
        out_specs=[vmem] * 4,
        out_shape=[jax.ShapeDtypeStruct(sends[o].shape, F32) for o in OPPOSITE],
        scratch_shapes=[pltpu.SemaphoreType.DMA((4,)), pltpu.SemaphoreType.DMA((4,))],
        compiler_params=pltpu.CompilerParams(collective_id=turn, has_side_effects=True),
        name="exchange",
    )(*sends)


def shards(depth, discharge, bed, friction, tile_ids, neighbors, moves):
    slots, tile = depth.shape[:2]
    owner_id = lax.axis_index("gx") * lax.axis_size("gy") + lax.axis_index("gy")
    base = owner_id * slots
    plan = moves[0]
    slot_id = jnp.arange(slots)
    group = group_of(slots, 4)
    together = slot_id[None] % group == slot_id[:, None] % group
    earlier = together & (slot_id[None] <= slot_id[:, None])

    leave = jnp.where(plan[:, :, 0] >= 0, plan[:, :, 0] - base, slots)
    land = jnp.where(plan[:, :, 1] >= 0, plan[:, :, 1] - base, slots)
    chosen = jnp.minimum(leave, slots - 1)
    to_low, to_high = bundle(chosen[0], chosen[1], depth, discharge, bed, friction)
    from_low = neighbour(to_high, "gy", -1)
    from_high = neighbour(to_low, "gy", 1)

    left = jnp.any(slot_id[:, None, None] == leave[None], (1, 2))
    lands = slot_id[:, None, None] == land[None]
    arrive = jnp.any(lands, 2)
    movers = plan.shape[1]
    entry = jnp.sum(jnp.where(lands, jnp.arange(movers)[None, None], 0), 2)
    mode = jnp.where(arrive[:, 0], 1, jnp.where(arrive[:, 1], 2, jnp.where(left, 3, 0)))

    def carried(used, value):
        seen = jnp.max(
            jnp.where(used[None] & earlier, slot_id[None], -1), 1
        )
        return jnp.sum(jnp.where(seen[:, None] == slot_id[None], value[None], 0), 1)

    own = carried(mode == 0, slot_id)
    low = carried(arrive[:, 0], entry[:, 0])
    high = carried(arrive[:, 1], entry[:, 1])

    links = neighbors.T
    remote = (links >= 0) & (links // slots != owner_id)
    rank = jnp.sum(remote[:, None, :] & (links[:, None, :] < links[:, :, None]), 2)
    link = jnp.where(remote, slots + rank, jnp.where(links >= 0, links - base, -1))
    before = jnp.sum(remote[:, None, :] & (slot_id[None, None] < slot_id[None, :, None]), 2)
    hit = remote[:, None, :] & (before[:, None, :] == jnp.arange(BLOCK_ROWS)[None, :, None])
    pick = jnp.sum(jnp.where(hit, slot_id[None, None], 0), 2)
    walls = jnp.broadcast_to(links[:, :, None], (4, slots, tile))
    as_int = lambda *xs: [x.astype(jnp.int32) for x in xs]
    mode, own, low, high, link, pick = as_int(mode, own, low, high, link, pick)

    h, q, z, n, edges, *sends = settle(
        group, mode, own, low, high, pick, depth, discharge, bed, friction, from_low, from_high
    )
    static = ()
    for turn in range(STEPS):
        first, last = turn == 0, turn == STEPS - 1
        gots = exchange(turn, sends)
        h, q, *rest = step(
            first, last, link, pick, tile_ids, (h, q, z, n), edges, gots, static, walls
        )
        if not last:
            edges, *sends = rest[:5]
            rest = rest[5:]
        static = (rest[0],) + (tuple(rest[1:3]) if first else static[1:])
    return h, q


def solution(mesh):
    return jax.shard_map(
        shards,
        mesh=mesh,
        in_specs=(
            P(("gx", "gy"), None, None),
            P(("gx", "gy"), None, None, None),
            P(("gx", "gy"), None, None),
            P(("gx", "gy"), None, None),
            P(("gx", "gy")),
            P(("gx", "gy"), None),
            P(("gx", "gy"), None, None, None),
        ),
        out_specs=(P(("gx", "gy"), None, None), P(("gx", "gy"), None, None, None)),
        check_vma=False,
    )
```
